256 devices in a mesh: noise: 8 (over x, core), sample: 32 (over y, z).
Axes of the slice: x: 4, y: 4, z: 8, core: 2. Of those that a mesh axis runs over, the one named last changes fastest.
Arguments:
- noise_latents: bfloat16 [16384, 256], P(('noise', 'sample')), may hold values from -18 to 18
- teacher_latent_rows: bfloat16 [32768, 256], P('sample', 'noise'), may hold values from -6 to 6
Outputs:
- noise_row_potential: float32 [16384], P('noise')
- column_potential: float32 [32768], P('sample')
- targets: bfloat16 [16384, 256], P(('noise', 'sample'))
The draws below stay inside these ranges and needn't reach their ends.
All inputs are finite; a program needn't handle non-finite values.
Results may differ from the reference program's by a relative error of at most 0.0039.
Values may be sent and summed in bfloat16 or wider, within the bound.
A program may use at most 64 MiB of HBM per device.

```python
import math
import jax
import jax.numpy as jnp
from jax import lax

EMBED_DIMENSION = 256
ITERS = 3
N = 16384
M = 32768


planted_count = 8


planted_level = 1.5


planted_offset = 0.45


def one_order(item_key):
    return jax.random.permutation(item_key, EMBED_DIMENSION)


def planted_pattern(key):
    index_key, sign_key, order_key = jax.random.split(key, 3)
    noise_pick = jax.random.permutation(jax.random.fold_in(index_key, 1), N)[:planted_count].astype(jnp.int32)
    teacher_pick = jax.random.permutation(jax.random.fold_in(index_key, 2), M // 2)[:planted_count].astype(jnp.int32)
    sign_rows = (jax.random.randint(sign_key, (planted_count, EMBED_DIMENSION), 0, 2) * 2 - 1).astype(jnp.float32)
    orders = jax.vmap(one_order)(jax.random.split(order_key, planted_count))
    balanced = jnp.where(orders < EMBED_DIMENSION // 2, 1.0, -1.0).astype(jnp.float32)
    return (noise_pick, teacher_pick, sign_rows, balanced)


def draw_noise_latents(key, part):
    noise_pick, teacher_pick, sign_rows, balanced = planted_pattern(key)
    key = jax.random.fold_in(key, 11)
    value_key = jax.random.fold_in(key, 0)
    strength_key = jax.random.fold_in(key, 2)
    value_entries = jnp.clip(jax.random.normal(value_key, (N, EMBED_DIMENSION), jnp.float32), -6.0, 6.0)
    offsets = jax.random.uniform(strength_key, (planted_count,), jnp.float32)
    strength = 3.2 + 1.6 * (jnp.arange(planted_count, dtype=jnp.float32) + offsets) / planted_count
    planted_rows = strength[:, None] * planted_level * sign_rows
    value_entries = value_entries.at[noise_pick].set(planted_rows)
    return value_entries.astype(jnp.bfloat16)


def draw_teacher_latent_rows(key, part):
    noise_pick, teacher_pick, sign_rows, balanced = planted_pattern(key)
    key = jax.random.fold_in(key, 23)
    value_key = jax.random.fold_in(key, 0)
    value_entries = jnp.clip(jax.random.normal(value_key, (M, EMBED_DIMENSION), jnp.float32), -6.0, 6.0)
    first_rows = planted_level * sign_rows
    second_rows = sign_rows * (planted_level + planted_offset * balanced)
    value_entries = value_entries.at[teacher_pick].set(first_rows)
    value_entries = value_entries.at[teacher_pick + M // 2].set(second_rows)
    return value_entries.astype(jnp.bfloat16)


def setup_inputs(seed: int = 0) -> dict:
    arg_keys = jax.random.split(jax.random.key(seed), 3)
    noise_latents = draw_noise_latents(jax.random.fold_in(arg_keys[2], 71), 0)
    teacher_latent_rows = draw_teacher_latent_rows(jax.random.fold_in(arg_keys[2], 71), 0)
    return {"noise_latents": noise_latents, "teacher_latent_rows": teacher_latent_rows}


smoothing_strength = 0.1


def reference(noise_latents, teacher_latent_rows):
    multiplier_coefficient = 1.0 / (EMBED_DIMENSION * smoothing_strength)
    block = math.gcd(N, 1024)
    count = N // block
    xn = jnp.sum(noise_latents.astype(jnp.float32) ** 2, axis=1)
    yn = jnp.sum(teacher_latent_rows.astype(jnp.float32) ** 2, axis=1)

    def price_submatrix(index):
        start = (index * block).astype(jnp.int32)
        rows = lax.dynamic_slice_in_dim(noise_latents, start, block, 0)
        norms = lax.dynamic_slice_in_dim(xn, start, block, 0)
        inner = jnp.dot(rows, teacher_latent_rows.T, preferred_element_type=jnp.float32)
        return (norms[:, None] + yn[None, :] - 2.0 * inner) * multiplier_coefficient

    indices = jnp.arange(count, dtype=jnp.int32)
    column_potential = jnp.zeros((M,), jnp.float32)
    noise_row_potential = jnp.zeros((N,), jnp.float32)
    for step in range(ITERS):
        def row_block(index):
            scores = column_potential[None, :] - price_submatrix(index)
            peak = jnp.max(scores, axis=1)
            return peak + jnp.log(jnp.sum(jnp.exp(scores - peak[:, None]), axis=1))

        noise_row_potential = -math.log(N) - lax.map(row_block, indices).reshape(N)

        def col_step(carry, index):
            peak, total = carry
            start = (index * block).astype(jnp.int32)
            part = lax.dynamic_slice_in_dim(noise_row_potential, start, block, 0)
            scores = part[:, None] - price_submatrix(index)
            new_peak = jnp.maximum(peak, jnp.max(scores, axis=0))
            total = total * jnp.exp(peak - new_peak) + jnp.sum(jnp.exp(scores - new_peak[None, :]), axis=0)
            return (new_peak, total), None

        init = (jnp.full((M,), -jnp.inf, jnp.float32), jnp.zeros((M,), jnp.float32))
        (peak, total), unused = lax.scan(col_step, init, indices)
        column_potential = -math.log(M) - (peak + jnp.log(total))

    def goal_submatrix(index):
        start = (index * block).astype(jnp.int32)
        part = lax.dynamic_slice_in_dim(noise_row_potential, start, block, 0)
        plan = jnp.exp(part[:, None] + column_potential[None, :] - price_submatrix(index))
        mass = jnp.sum(plan, axis=1)
        numer = jnp.dot(plan.astype(jnp.bfloat16), teacher_latent_rows, preferred_element_type=jnp.float32)
        return (numer / mass[:, None]).astype(jnp.bfloat16)

    targets = lax.map(goal_submatrix, indices).reshape(N, EMBED_DIMENSION)
    return noise_row_potential, column_potential, targets
```

```python
import functools
import math

import jax
import jax.numpy as jnp
from jax import lax
from jax.experimental import pallas as pl
from jax.experimental.pallas import tpu as pltpu
from jax.sharding import PartitionSpec as P

ITERS = 3
WIDTH = 256
ROWS, COLS = 16384, 32768
STRENGTH = 0.1
NX, NY, NZ, NC = 4, 4, 8, 2
GROUP = 16
SHARE = 64
BLOCK_ROWS = GROUP * SHARE
PIECE = 256
CUT = 128
CUTS = BLOCK_ROWS // CUT
TILES = NZ * PIECE // 128
MESH = pl.DeviceIdType.MESH
F32, BF16 = jnp.float32, jnp.bfloat16
LN2 = math.log(2.0)
COST = 1.0 / (WIDTH * STRENGTH)


def place(x, c, y, z):
    return (x * NC + c, y * NZ + z)


def spread(row):
    return jnp.broadcast_to(row, (128, 128)).T


def kernel(noise_ref, teach_ref, row_out, col_out, target_out, slices, cols, rows_x, tall, score, peak, total,
           gain, beta, plan, row_box, col_box, row_pot, col_pot, mine, boxes,
           sa, ra, sx, rx, sz, rz, sc, rc, srow, rrow, scol, rcol, sn, rn, so, ro, sp, rp):
    n, s = lax.axis_index("noise"), lax.axis_index("sample")
    x, c = n // NC, n % NC
    y, z = s // NZ, s % NZ
    me = x * NY + y
    other = 1 - c
    slot = z * NC + c

    def xy(k):
        px, py = (x + k // NY) % NX, (y + k % NY) % NY
        return px * NY + py, place(px, c, py, z)

    def zc(k):
        pz, pc = (z + k // NC) % NZ, (c + k % NC) % NC
        return pz * NC + pc, place(x, pc, y, pz)

    barrier = pltpu.get_barrier_semaphore()

    def greet(k, carry):
        pl.semaphore_signal(barrier, inc=1, device_id=xy(k)[1], device_id_type=MESH)
        pl.semaphore_signal(barrier, inc=1, device_id=zc(k)[1], device_id_type=MESH)
        return carry

    lax.fori_loop(1, GROUP, greet, 0)

    row_id = lax.broadcasted_iota(jnp.int32, (32, 32), 0)
    col_id = lax.broadcasted_iota(jnp.int32, (32, 32), 1)
    eye = jnp.where(row_id == col_id, 1.0, 0.0).astype(BF16)
    for q in range(NX):
        part = lax.dot_general(eye, teach_ref[q * PIECE:(q + 1) * PIECE, :], (((1,), (1,)), ((), ())),
                               preferred_element_type=F32)
        slices[q] = part.astype(BF16)
    rows_x[me] = noise_ref[...]
    cols[z, x, c] = slices[x]

    pl.semaphore_wait(barrier, 2 * (GROUP - 1))

    def quarter(k):
        px = (x + k) % NX
        return px, pltpu.make_async_remote_copy(
            src_ref=slices.at[px], dst_ref=cols.at[z, x, c], send_sem=sa.at[px], recv_sem=ra.at[x],
            device_id=place(px, c, y, z), device_id_type=MESH)

    def quarter_in(k):
        px = (x + k) % NX
        return pltpu.make_async_remote_copy(
            src_ref=slices.at[px], dst_ref=cols.at[z, px, c], send_sem=sa.at[px], recv_sem=ra.at[px],
            device_id=place(px, c, y, z), device_id_type=MESH)

    for k in range(1, NX):
        quarter(k)[1].start()

    def noise_copy(k, incoming):
        p, device = xy(k)
        at = p if incoming else me
        return pltpu.make_async_remote_copy(
            src_ref=rows_x.at[me], dst_ref=rows_x.at[at], send_sem=sx.at[p], recv_sem=rx.at[at],
            device_id=device, device_id_type=MESH)

    def noise_start(k, carry):
        noise_copy(k, False).start()
        return carry

    lax.fori_loop(1, GROUP, noise_start, 0)
    for k in range(1, NX):
        quarter_in(k).wait_recv()

    def piece_copy(d, incoming):
        pz = (z + d) % NZ
        at = pz if incoming else z
        return pltpu.make_async_remote_copy(
            src_ref=cols.at[z, :, c], dst_ref=cols.at[at, :, c], send_sem=sz.at[pz], recv_sem=rz.at[at],
            device_id=place(x, c, y, pz), device_id_type=MESH)

    def core_copy(pz, incoming):
        at = other if incoming else c
        return pltpu.make_async_remote_copy(
            src_ref=cols.at[pz, :, c], dst_ref=cols.at[pz, :, at], send_sem=sc.at[pz], recv_sem=rc.at[pz],
            device_id=place(x, other, y, z), device_id_type=MESH)

    def away(k):
        return ((k + 1) // 2) * (2 * (k % 2) - 1) + NZ

    def piece_start(k, carry):
        piece_copy(away(k) % NZ, False).start()
        return carry

    lax.fori_loop(1, NZ, piece_start, 0)

    peak[...] = jnp.full((BLOCK_ROWS, 128), -1e30, F32)
    total[...] = jnp.zeros((BLOCK_ROWS, 128), F32)

    def noise_wait(k, carry):
        noise_copy(k, True).wait_recv()
        return carry

    lax.fori_loop(1, GROUP, noise_wait, 0)

    def scores_of(pz):
        block = cols[pz].reshape(WIDTH, PIECE)
        wide = block.astype(F32)
        norms = jnp.sum(wide * wide, axis=0, keepdims=True) * (COST / LN2)
        for b in range(CUTS):
            r = pl.ds(b * CUT, CUT)
            latents = rows_x[2 * b:2 * b + 2].reshape(CUT, WIDTH)
            dots = jnp.dot(latents, block, preferred_element_type=F32)
            h = dots * (2.0 * COST / LN2) - norms
            score[pz, r, :] = h
            left, right = h[:, :128], h[:, 128:]
            old = peak[r, :]
            new = jnp.maximum(old, jnp.maximum(left, right))
            total[r, :] = total[r, :] * jnp.exp2(old - new) + (jnp.exp2(left - new) + jnp.exp2(right - new))
            peak[r, :] = new

    def piece(k, carry):
        @pl.when(k < NZ)
        def _():
            d = away(k) % NZ
            pz = (z + d) % NZ

            @pl.when(k > 0)
            def _():
                piece_copy(d, True).wait_recv()

            core_copy(pz, False).start()

        @pl.when(k > 0)
        def _():
            pz = (z + away(k - 1)) % NZ
            core_copy(pz, True).wait_recv()
            scores_of(pz)

        return carry

    lax.fori_loop(0, NZ + 1, piece, 0)

    def row_copy(turn, k, incoming):
        p, device = xy(k)
        at = p if incoming else me
        return pltpu.make_async_remote_copy(
            src_ref=row_box.at[turn, me], dst_ref=row_box.at[turn, at], send_sem=srow.at[turn, p],
            recv_sem=rrow.at[turn, at], device_id=device, device_id_type=MESH)

    def row_start(turn):
        def start(k, carry):
            row_copy(turn, k, False).start()
            return carry

        lax.fori_loop(1, GROUP, start, 0)

    def row_wait(turn):
        def wait(k, carry):
            row_copy(turn, k, True).wait_recv()
            return carry

        lax.fori_loop(1, GROUP, wait, 0)

    def col_copy(turn, k, incoming):
        p, device = zc(k)
        at = p if incoming else slot
        return pltpu.make_async_remote_copy(
            src_ref=col_box.at[turn, slot], dst_ref=col_box.at[turn, at], send_sem=scol.at[turn, p],
            recv_sem=rcol.at[turn, at], device_id=device, device_id_type=MESH)

    def col_trade(turn):
        def start(k, carry):
            col_copy(turn, k, False).start()
            return carry

        lax.fori_loop(1, GROUP, start, 0)

        def wait(k, carry):
            col_copy(turn, k, True).wait_recv()
            return carry

        lax.fori_loop(1, GROUP, wait, 0)

    for b in range(CUTS):
        r = pl.ds(b * CUT, CUT)
        lane_peak = peak[r, :].T
        lane_total = total[r, :].T
        top = jnp.max(lane_peak, axis=0, keepdims=True)
        sums = jnp.sum(lane_total * jnp.exp2(lane_peak - top), axis=0, keepdims=True)
        row_box[0, me, b:b + 1, :] = top + jnp.log(sums) * (1.0 / LN2)
    row_start(0)
    for pz in range(NZ):
        block = cols[pz].reshape(WIDTH, PIECE).astype(F32)
        tall[pz * PIECE:(pz + 1) * PIECE, :] = block.T.astype(BF16)
    for b in range(CUTS):
        latents = rows_x[2 * b:2 * b + 2].reshape(CUT, WIDTH).astype(F32)
        squares = latents * latents
        mine[0, b:b + 1, :] = jnp.sum((squares[:, :128] + squares[:, 128:]).T, axis=0, keepdims=True)
    row_wait(0)
    lse = row_box[0]
    top = jnp.max(lse, axis=0)
    row_log = -math.log2(ROWS) - (top + jnp.log(jnp.sum(jnp.exp2(lse - top), axis=0)) * (1.0 / LN2))

    mine[1] = row_log

    def first_column(b, carry):
        r = pl.ds(pl.multiple_of(b * CUT, CUT), CUT)
        shift = spread(mine[1, pl.ds(b, 1), :])
        for t in range(TILES):
            lanes = pl.ds((t % 2) * 128, 128)
            h = score[t // 2, r, lanes] + shift
            top = jnp.max(h, axis=0, keepdims=True)
            e = jnp.exp2(h - top)
            score[t // 2, r, lanes] = e
            gain[b, t:t + 1, :] = top
            beta[b, t:t + 1, :] = jnp.sum(e, axis=0, keepdims=True)
        return carry

    lax.fori_loop(0, CUTS, first_column, 0)
    cut_peak = gain[...]
    top = jnp.max(cut_peak, axis=0)
    sums = jnp.sum(beta[...] * jnp.exp2(cut_peak - top), axis=0)
    col_box[0, slot] = top + jnp.log(sums) * (1.0 / LN2)
    col_trade(0)
    lse = col_box[0]
    top = jnp.max(lse, axis=0)
    col_log = -math.log2(COLS) - (top + jnp.log(jnp.sum(jnp.exp2(lse - top), axis=0)) * (1.0 / LN2))
    gain[...] = jnp.exp2(cut_peak + col_log)
    beta[...] = gain[...]

    alpha = None
    for turn in range(1, ITERS):
        def row_sums(b, carry):
            r = pl.ds(pl.multiple_of(b * CUT, CUT), CUT)
            acc = None
            for t in range(TILES):
                term = score[t // 2, r, (t % 2) * 128:(t % 2) * 128 + 128] * beta[b, t:t + 1, :]
                acc = term if acc is None else acc + term
            row_box[turn, me, pl.ds(b, 1), :] = jnp.sum(acc.T, axis=0, keepdims=True)
            return carry

        lax.fori_loop(0, CUTS, row_sums, 0)
        row_start(turn)
        row_wait(turn)
        alpha = 1.0 / (ROWS * jnp.sum(row_box[turn], axis=0))
        mine[2] = alpha

        def col_sums(b, carry):
            r = pl.ds(pl.multiple_of(b * CUT, CUT), CUT)
            weight = spread(mine[2, pl.ds(b, 1), :])
            out = []
            for t in range(TILES):
                term = score[t // 2, r, (t % 2) * 128:(t % 2) * 128 + 128] * weight
                out.append(carry[t] + jnp.sum(term.reshape(CUT // 8, 8, 128), axis=0) * gain[b, t:t + 1, :])
            return tuple(out)

        sums = lax.fori_loop(0, CUTS, col_sums, tuple(jnp.zeros((8, 128), F32) for _ in range(TILES)))
        for t in range(TILES):
            col_box[turn, slot, t:t + 1, :] = jnp.sum(sums[t], axis=0, keepdims=True)
        col_trade(turn)
        factor = 1.0 / (COLS * jnp.sum(col_box[turn], axis=0))
        beta[...] = gain[...] * factor

    row_pot[z] = COST * mine[0] + LN2 * (row_log + jnp.log(alpha) * (1.0 / LN2))
    col_pot[x] = LN2 * (col_log + jnp.log(factor) * (1.0 / LN2))

    def row_pot_copy(d, incoming):
        pz = (z + d) % NZ
        at = pz if incoming else z
        return pltpu.make_async_remote_copy(
            src_ref=row_pot.at[z], dst_ref=row_pot.at[at], send_sem=so.at[pz], recv_sem=ro.at[at],
            device_id=place(x, c, y, pz), device_id_type=MESH)

    def col_pot_copy(d, incoming):
        px = (x + d) % NX
        at = px if incoming else x
        return pltpu.make_async_remote_copy(
            src_ref=col_pot.at[x], dst_ref=col_pot.at[at], send_sem=sp.at[px], recv_sem=rp.at[at],
            device_id=place(px, c, y, z), device_id_type=MESH)

    def row_pot_start(d, carry):
        row_pot_copy(d, False).start()
        return carry

    def col_pot_start(d, carry):
        col_pot_copy(d, False).start()
        return carry

    lax.fori_loop(1, NZ, row_pot_start, 0)
    lax.fori_loop(1, NX, col_pot_start, 0)

    def sum_copy(p, device, incoming):
        at = p if incoming else me
        return pltpu.make_async_remote_copy(
            src_ref=boxes.at[0, p], dst_ref=boxes.at[1, at], send_sem=sn.at[p], recv_sem=rn.at[at],
            device_id=device, device_id_type=MESH)

    def project(step, carry):
        px = (x + 1 + step) % NX
        for half in range(2):
            b = px * 2 + half
            r = pl.ds(pl.multiple_of(b * CUT, CUT), CUT)
            weight = spread(mine[2, pl.ds(b, 1), :])
            acc = None
            for t in range(TILES):
                p = score[t // 2, r, (t % 2) * 128:(t % 2) * 128 + 128] * weight * beta[b, t:t + 1, :]
                acc = p if acc is None else acc + p
                plan[half * CUT:half * CUT + CUT, t * 128:t * 128 + 128] = p.astype(BF16)
            row_box[ITERS, me, pl.ds(b, 1), :] = jnp.sum(acc.T, axis=0, keepdims=True)
        numer = jnp.dot(plan[...], tall[...], preferred_element_type=F32).astype(BF16)
        for py in range(NY):
            p = px * NY + py
            boxes[0, p] = numer[py * SHARE:(py + 1) * SHARE, :]

            @pl.when(p != me)
            def _():
                sum_copy(p, place(px, c, py, z), False).start()

        return carry

    lax.fori_loop(0, NX, project, 0)
    row_start(ITERS)
    boxes[1, me] = boxes[0, me]

    def col_pot_wait(d, carry):
        col_pot_copy(d, True).wait_recv()
        return carry

    def row_pot_wait(d, carry):
        row_pot_copy(d, True).wait_recv()
        return carry

    lax.fori_loop(1, NX, col_pot_wait, 0)
    for px in range(NX):
        for half in range(2):
            col_out[2 * px + half:2 * px + half + 1, :] = col_pot[px, pl.ds(2 * z + half, 1), :]
    lax.fori_loop(1, NZ, row_pot_wait, 0)
    low = lax.broadcasted_iota(jnp.int32, (1, 128), 1) < SHARE
    for py in range(NY):
        for pair in range(NZ // 2):
            even = row_pot[2 * pair, pl.ds(2 * x + py // 2, 1), :]
            odd = row_pot[2 * pair + 1, pl.ds(2 * x + py // 2, 1), :]
            if py % 2:
                even = pltpu.roll(even, SHARE, 1)
            else:
                odd = pltpu.roll(odd, SHARE, 1)
            row_out[4 * py + pair:4 * py + pair + 1, :] = jnp.where(low, even, odd)

    row_wait(ITERS)
    mine[3] = jnp.sum(row_box[ITERS], axis=0)
    total[0:128, :] = spread(mine[3, pl.ds(me // 2, 1), :])
    mass = total[pl.ds(pl.multiple_of((me % 2) * SHARE, SHARE), SHARE), :]

    def sum_wait(k, carry):
        p, device = xy(k)
        sum_copy(p, device, True).wait_recv()
        return carry

    lax.fori_loop(1, GROUP, sum_wait, 0)
    numer = jnp.sum(boxes[1].astype(F32), axis=0)
    target_out[:, :128] = (numer[:, :128] / mass).astype(BF16)
    target_out[:, 128:] = (numer[:, 128:] / mass).astype(BF16)

    for k in range(1, NX):
        quarter(k)[1].wait_send()

    def drain(k, carry):
        p, device = xy(k)
        noise_copy(k, False).wait_send()
        sum_copy(p, device, False).wait_send()
        for turn in range(ITERS + 1):
            row_copy(turn, k, False).wait_send()
        for turn in range(ITERS):
            col_copy(turn, k, False).wait_send()
        return carry

    lax.fori_loop(1, GROUP, drain, 0)

    def drain_z(d, carry):
        piece_copy(d, False).wait_send()
        row_pot_copy(d, False).wait_send()
        return carry

    lax.fori_loop(1, NZ, drain_z, 0)

    def drain_core(d, carry):
        core_copy(d, False).wait_send()
        return carry

    lax.fori_loop(0, NZ, drain_core, 0)

    def drain_x(d, carry):
        col_pot_copy(d, False).wait_send()
        return carry

    lax.fori_loop(1, NX, drain_x, 0)


def shards(noise_latents, teacher_latent_rows):
    vmem = pl.BlockSpec(memory_space=pltpu.VMEM)
    dma = pltpu.SemaphoreType.DMA
    row_pot, col_pot, targets = pl.pallas_call(
        kernel,
        out_shape=(
            jax.ShapeDtypeStruct((16, 128), F32),
            jax.ShapeDtypeStruct((8, 128), F32),
            jax.ShapeDtypeStruct((SHARE, WIDTH), BF16),
        ),
        in_specs=[vmem, vmem],
        out_specs=(vmem, vmem, vmem),
        scratch_shapes=[
            pltpu.VMEM((NX, 32, PIECE), BF16),
            pltpu.VMEM((NZ, NX, NC, 32, PIECE), BF16),
            pltpu.VMEM((GROUP, SHARE, WIDTH), BF16),
            pltpu.VMEM((NZ * PIECE, WIDTH), BF16),
            pltpu.VMEM((NZ, BLOCK_ROWS, PIECE), F32),
            pltpu.VMEM((BLOCK_ROWS, 128), F32),
            pltpu.VMEM((BLOCK_ROWS, 128), F32),
            pltpu.VMEM((CUTS, TILES, 128), F32),
            pltpu.VMEM((CUTS, TILES, 128), F32),
            pltpu.VMEM((2 * CUT, NZ * PIECE), BF16),
            pltpu.VMEM((ITERS + 1, GROUP, 8, 128), F32),
            pltpu.VMEM((ITERS, GROUP, TILES, 128), F32),
            pltpu.VMEM((NZ, 8, 128), F32),
            pltpu.VMEM((NX, TILES, 128), F32),
            pltpu.VMEM((4, 8, 128), F32),
            pltpu.VMEM((2, GROUP, SHARE, WIDTH), BF16),
            dma((NX,)), dma((NX,)),
            dma((GROUP,)), dma((GROUP,)),
            dma((NZ,)), dma((NZ,)),
            dma((NZ,)), dma((NZ,)),
            dma((ITERS + 1, GROUP)), dma((ITERS + 1, GROUP)),
            dma((ITERS, GROUP)), dma((ITERS, GROUP)),
            dma((GROUP,)), dma((GROUP,)),
            dma((NZ,)), dma((NZ,)),
            dma((NX,)), dma((NX,)),
        ],
        compiler_params=pltpu.CompilerParams(
            collective_id=0, has_side_effects=True, vmem_limit_bytes=48 * 2**20),
        name="sinkhorn",
    )(noise_latents, teacher_latent_rows)
    return row_pot.reshape(2048), col_pot.reshape(1024), targets


def solution(mesh):
    return jax.shard_map(
        shards,
        mesh=mesh,
        in_specs=(P(("noise", "sample"), None), P("sample", "noise")),
        out_specs=(P("noise"), P("sample"), P(("noise", "sample"), None)),
        check_vma=False,
    )
```

```python
import math

import jax
import jax.numpy as jnp
from jax import lax
from jax.experimental import pallas as pl
from jax.experimental.pallas import tpu as pltpu
from jax.sharding import PartitionSpec as P

ITERS = 3
WIDTH = 256
ROWS, COLS = 16384, 32768
STRENGTH = 0.1
NX, NY, NZ, NC = 4, 4, 8, 2
GROUP = NX * NY
SHARE = 64
BLOCK_ROWS = GROUP * SHARE
PIECE = 256
CUT = 128
CUTS = BLOCK_ROWS // CUT
TILES = NZ * PIECE // 128
MESH = pl.DeviceIdType.MESH
F32, BF16 = jnp.float32, jnp.bfloat16
LN2 = math.log(2.0)
COST = 1.0 / (WIDTH * STRENGTH)


def spread(row):
    return jnp.broadcast_to(row, (128, 128)).T


def log2(a):
    return jnp.log(a) * (1.0 / LN2)


def lanes_of(t):
    return slice((t % 2) * 128, (t % 2) * 128 + 128)


def kernel(noise_hbm, teach_hbm, row_out, col_out, target_out, slices, cols, rows_x, tall, score, peak, total,
           gain, beta, plan, row_box, col_box, core_box, row_pot, col_pot, mine, mass_box, boxes,
           load, sa, ra, sx, rx, sz, rz, sc, rc, srow, rrow, scol, rcol, score_s, score_r, sm, rm, sn, rn, so, ro, sp, rp):
    n, s = lax.axis_index("noise"), lax.axis_index("sample")
    x, c = lax.div(n, NC), lax.rem(n, NC)
    y, z = lax.div(s, NZ), lax.rem(s, NZ)
    me = x * NY + y
    other = 1 - c
    xs = [x] + [lax.rem(x + d, NX) for d in range(1, NX)]
    ys = [y] + [lax.rem(y + d, NY) for d in range(1, NY)]
    zs = [z] + [lax.rem(z + d, NZ) for d in range(1, NZ)]
    noise_at = [px * NC + c for px in xs]
    across = [py * NZ + z for py in ys]
    along = [y * NZ + pz for pz in zs]
    sibling = (x * NC + other, s)
    near = [1, 7, 2, 6, 3, 5, 4]
    xy = [(noise_at[k // NY], across[k % NY]) for k in range(1, GROUP)]

    def send(src, dst, send_sem, recv_sem, device):
        pltpu.make_async_remote_copy(src_ref=src, dst_ref=dst, send_sem=send_sem, recv_sem=recv_sem,
                                     device_id=device, device_id_type=MESH).start()

    def wait(ref, sem):
        pltpu.make_async_copy(ref, ref, sem).wait()

    loads = [pltpu.make_async_copy(teach_hbm.at[:, q * PIECE:(q + 1) * PIECE], slices.at[q], load.at[q])
             for q in range(NX)]
    loads.append(pltpu.make_async_copy(noise_hbm, rows_x.at[me], load.at[NX]))
    for copy in loads:
        copy.start()

    barrier = pltpu.get_barrier_semaphore()
    greeted = xy + [(n, along[d]) for d in range(1, NZ)] + [sibling]
    for device in greeted:
        pl.semaphore_signal(barrier, inc=1, device_id=device, device_id_type=MESH)
    peak[...] = jnp.full((BLOCK_ROWS, 128), -1e30, F32)
    total[...] = jnp.zeros((BLOCK_ROWS, 128), F32)
    for copy in loads:
        copy.wait()
    cols[z, x, c] = slices[x]
    pl.semaphore_wait(barrier, len(greeted))

    for d in range(1, NX):
        send(slices.at[xs[d]], cols.at[z, x, c], sa.at[0], ra.at[0], (noise_at[d], s))
    for device in xy:
        send(rows_x.at[me], rows_x.at[me], sx.at[0], rx.at[0], device)
    wait(slices.at[0:NX - 1], ra.at[0])

    for d in near:
        send(cols.at[z, :, c], cols.at[z, :, c], sz.at[0], rz.at[z], (n, along[d]))
    send(cols.at[z, :, c], cols.at[z, :, c], sc.at[0], rc.at[z], sibling)
    wait(rows_x.at[0:GROUP - 1], rx.at[0])

    def scores_of(pz):
        block = cols[pz].reshape(WIDTH, PIECE)
        wide = block.astype(F32)
        norms = jnp.sum(wide * wide, axis=0, keepdims=True) * (COST / LN2)
        for b in range(CUTS):
            r = slice(b * CUT, (b + 1) * CUT)
            latents = rows_x[2 * b:2 * b + 2].reshape(CUT, WIDTH)
            dots = jnp.dot(latents, block, preferred_element_type=F32)
            h = dots * (2.0 * COST / LN2) - norms
            score[pz, r, :] = h
            left, right = h[:, :128], h[:, 128:]
            old = peak[r, :]
            new = jnp.maximum(old, jnp.maximum(left, right))
            total[r, :] = total[r, :] * jnp.exp2(old - new) + (jnp.exp2(left - new) + jnp.exp2(right - new))
            peak[r, :] = new

    def away(k):
        return lax.div(k + 1, 2) * (2 * lax.rem(k, 2) - 1) + NZ

    def piece(k, carry):
        @pl.when(k < NZ)
        def _():
            pz = lax.rem(z + away(k), NZ)
            wait(cols.at[pz, :, c], rz.at[pz])
            send(cols.at[pz, :, c], cols.at[pz, :, c], sc.at[0], rc.at[pz], sibling)

        pz = lax.rem(z + away(k - 1), NZ)
        wait(cols.at[pz, :, other], rc.at[pz])
        scores_of(pz)
        return carry

    lax.fori_loop(1, NZ + 1, piece, 0)

    def row_start(turn):
        for device in xy:
            send(row_box.at[turn, me], row_box.at[turn, me], srow.at[turn], rrow.at[turn], device)

    def row_wait(turn):
        wait(row_box.at[turn, 0:GROUP - 1], rrow.at[turn])

    def col_start(turn):
        for d in near:
            send(col_box.at[turn, z], col_box.at[turn, z], scol.at[turn], rcol.at[turn], (n, along[d]))

    def col_wait(turn):
        wait(col_box.at[turn, 0:NZ - 1], rcol.at[turn])

    def core_trade(turn, value):
        core_box[turn, c] = value
        send(core_box.at[turn, c], core_box.at[turn, c], score_s.at[turn], score_r.at[turn], sibling)
        wait(core_box.at[turn, other], score_r.at[turn])
        return core_box[turn]

    def log_sum(logs):
        top = jnp.max(logs, axis=0)
        return top + log2(jnp.sum(jnp.exp2(logs - top), axis=0))

    for b in range(CUTS):
        r = slice(b * CUT, (b + 1) * CUT)
        lane_peak = peak[r, :].T
        lane_total = total[r, :].T
        top = jnp.max(lane_peak, axis=0, keepdims=True)
        sums = jnp.sum(lane_total * jnp.exp2(lane_peak - top), axis=0, keepdims=True)
        row_box[0, me, b:b + 1, :] = top + log2(sums)
    row_start(0)
    for pz in range(NZ):
        block = cols[pz].reshape(WIDTH, PIECE).astype(F32)
        tall[pz * PIECE:(pz + 1) * PIECE, :] = block.T.astype(BF16)
    for b in range(CUTS):
        latents = rows_x[2 * b:2 * b + 2].reshape(CUT, WIDTH).astype(F32)
        squares = latents * latents
        mine[0, b:b + 1, :] = jnp.sum((squares[:, :128] + squares[:, 128:]).T, axis=0, keepdims=True)
    row_wait(0)
    row_log = -math.log2(ROWS) - log_sum(row_box[0])

    mine[1] = row_log

    def first_column(b, carry):
        r = pl.ds(pl.multiple_of(b * CUT, CUT), CUT)
        shift = spread(mine[1, pl.ds(b, 1), :])
        for t in range(TILES):
            h = (score[t // 2, r, lanes_of(t)] + shift).reshape(CUT // 8, 8, 128)
            top = jnp.max(h, axis=0)
            e = jnp.exp2(h - top)
            score[t // 2, r, lanes_of(t)] = e.reshape(CUT, 128)
            gain[b, t] = top
            beta[b, t] = jnp.sum(e, axis=0)
        return carry

    lax.fori_loop(0, CUTS, first_column, 0)
    for t in range(TILES):
        cut_peak = gain[:, t]
        top = jnp.max(jnp.max(cut_peak, axis=0), axis=0, keepdims=True)
        sums = jnp.sum(jnp.sum(beta[:, t] * jnp.exp2(cut_peak - top), axis=0), axis=0, keepdims=True)
        col_box[0, z, t:t + 1, :] = top + log2(sums)
    col_start(0)
    col_wait(0)
    col_log = -math.log2(COLS) - log_sum(core_trade(0, log_sum(col_box[0])))
    for t in range(TILES):
        start_gain = jnp.exp2(gain[:, t] + col_log[t:t + 1, :])
        gain[:, t] = start_gain
        beta[:, t] = start_gain

    alpha = None
    for turn in range(1, ITERS):
        for b in range(CUTS):
            r = slice(b * CUT, (b + 1) * CUT)
            acc = None
            for t in range(TILES):
                term = score[t // 2, r, lanes_of(t)].reshape(CUT // 8, 8, 128) * beta[b, t]
                acc = term if acc is None else acc + term
            row_box[turn, me, b:b + 1, :] = jnp.sum(acc.reshape(CUT, 128).T, axis=0, keepdims=True)
        row_start(turn)
        row_wait(turn)
        alpha = 1.0 / (ROWS * jnp.sum(row_box[turn], axis=0))
        mine[2] = alpha

        sums = [None] * TILES
        for b in range(CUTS):
            r = slice(b * CUT, (b + 1) * CUT)
            weight = spread(alpha[b:b + 1, :])
            for t in range(TILES):
                term = score[t // 2, r, lanes_of(t)] * weight
                term = jnp.sum(term.reshape(CUT // 8, 8, 128), axis=0) * gain[b, t]
                sums[t] = term if b == 0 else sums[t] + term
        for t in range(TILES):
            col_box[turn, z, t:t + 1, :] = jnp.sum(sums[t], axis=0, keepdims=True)
        col_start(turn)
        col_wait(turn)
        pair = core_trade(turn, jnp.sum(col_box[turn], axis=0))
        factor = 1.0 / (COLS * (pair[0] + pair[1]))
        for t in range(TILES):
            beta[:, t] = gain[:, t] * factor[t:t + 1, :]

    row_pot[z] = COST * mine[0] + LN2 * (row_log + log2(alpha))
    col_pot[x] = LN2 * (col_log + log2(factor))
    for d in near:
        send(row_pot.at[z], row_pot.at[z], so.at[0], ro.at[0], (n, along[d]))
    for d in range(1, NX):
        send(col_pot.at[x], col_pot.at[x], sp.at[0], rp.at[0], (noise_at[d], s))

    def project(px, peers):
        for half in range(2):
            b = px * 2 + half
            r = pl.ds(pl.multiple_of(b * CUT, CUT), CUT)
            weight = spread(mine[2, pl.ds(b, 1), :])
            acc = None
            for t in range(TILES):
                p = (score[t // 2, r, lanes_of(t)] * weight).reshape(CUT // 8, 8, 128) * beta[b, t]
                acc = p if acc is None else acc + p
                plan[half * CUT:half * CUT + CUT, t * 128:t * 128 + 128] = p.reshape(CUT, 128).astype(BF16)
            mass_box[0, px, half:half + 1, :] = jnp.sum(acc.reshape(CUT, 128).T, axis=0, keepdims=True)
        numer = jnp.dot(plan[...], tall[...], preferred_element_type=F32).astype(BF16)
        for py in range(NY):
            boxes[0, px * NY + py] = numer[py * SHARE:(py + 1) * SHARE, :]
        for d, device in peers:
            send(mass_box.at[0, px], mass_box.at[1, me], sm.at[0], rm.at[0], device)
            send(boxes.at[0, px * NY + ys[d]], boxes.at[1, me], sn.at[0], rn.at[0], device)

    for k in range(1, NX):
        project(xs[k], [(d, (noise_at[k], across[d])) for d in range(NY)])
    project(x, [(d, (n, across[d])) for d in range(1, NY)])
    boxes[1, me] = boxes[0, me]
    mass_box[1, me] = mass_box[0, x]

    wait(col_pot.at[0:NX - 1], rp.at[0])
    for px in range(NX):
        for half in range(2):
            col_out[2 * px + half:2 * px + half + 1, :] = col_pot[px, pl.ds(2 * z + half, 1), :]
    wait(row_pot.at[0:NZ - 1], ro.at[0])
    low = lax.broadcasted_iota(jnp.int32, (1, 128), 1) < SHARE
    for py in range(NY):
        for pair in range(NZ // 2):
            even = row_pot[2 * pair, pl.ds(2 * x + py // 2, 1), :]
            odd = row_pot[2 * pair + 1, pl.ds(2 * x + py // 2, 1), :]
            if py % 2:
                even = pltpu.roll(even, SHARE, 1)
            else:
                odd = pltpu.roll(odd, SHARE, 1)
            row_out[4 * py + pair:4 * py + pair + 1, :] = jnp.where(low, even, odd)

    wait(mass_box.at[1, 0:GROUP - 1], rm.at[0])
    mine[3] = jnp.sum(mass_box[1], axis=0)
    total[0:128, :] = spread(mine[3, pl.ds(lax.div(y, 2), 1), :])
    mass = total[pl.ds(pl.multiple_of(lax.rem(y, 2) * SHARE, SHARE), SHARE), :]
    wait(boxes.at[1, 0:GROUP - 1], rn.at[0])
    numer = jnp.sum(boxes[1].astype(F32), axis=0)
    target_out[:, :128] = (numer[:, :128] / mass).astype(BF16)
    target_out[:, 128:] = (numer[:, 128:] / mass).astype(BF16)

    wait(slices.at[0:NX - 1], sa.at[0])
    wait(rows_x.at[0:GROUP - 1], sx.at[0])
    wait(cols.at[0:NZ - 1, :, c], sz.at[0])
    wait(cols.at[:, :, c], sc.at[0])
    for turn in range(ITERS):
        wait(row_box.at[turn, 0:GROUP - 1], srow.at[turn])
        wait(col_box.at[turn, 0:NZ - 1], scol.at[turn])
        wait(core_box.at[turn, c], score_s.at[turn])
    wait(row_pot.at[0:NZ - 1], so.at[0])
    wait(col_pot.at[0:NX - 1], sp.at[0])
    wait(mass_box.at[1, 0:GROUP - 1], sm.at[0])
    wait(boxes.at[1, 0:GROUP - 1], sn.at[0])


def give(a, b, c, a_out, b_out, c_out, sems):
    copies = [pltpu.make_async_copy(src, dst, sems.at[k])
              for k, (src, dst) in enumerate(((a, a_out), (b, b_out), (c, c_out)))]
    for copy in copies:
        copy.start()
    for copy in copies:
        copy.wait()


def shards(noise_latents, teacher_latent_rows):
    vmem = pl.BlockSpec(memory_space=pltpu.VMEM)
    hbm = pl.BlockSpec(memory_space=pltpu.HBM)
    dma = pltpu.SemaphoreType.DMA
    shapes = (
        jax.ShapeDtypeStruct((16, 128), F32),
        jax.ShapeDtypeStruct((8, 128), F32),
        jax.ShapeDtypeStruct((SHARE, WIDTH), BF16),
    )
    results = pl.pallas_call(
        kernel,
        out_shape=shapes,
        in_specs=[hbm, hbm],
        out_specs=(vmem, vmem, vmem),
        scratch_shapes=[
            pltpu.VMEM((NX, 32, PIECE), BF16),
            pltpu.VMEM((NZ, NX, NC, 32, PIECE), BF16),
            pltpu.VMEM((GROUP, SHARE, WIDTH), BF16),
            pltpu.VMEM((NZ * PIECE, WIDTH), BF16),
            pltpu.VMEM((NZ, BLOCK_ROWS, PIECE), F32),
            pltpu.VMEM((BLOCK_ROWS, 128), F32),
            pltpu.VMEM((BLOCK_ROWS, 128), F32),
            pltpu.VMEM((CUTS, TILES, 8, 128), F32),
            pltpu.VMEM((CUTS, TILES, 8, 128), F32),
            pltpu.VMEM((2 * CUT, NZ * PIECE), BF16),
            pltpu.VMEM((ITERS, GROUP, 8, 128), F32),
            pltpu.VMEM((ITERS, NZ, TILES, 128), F32),
            pltpu.VMEM((ITERS, NC, TILES, 128), F32),
            pltpu.VMEM((NZ, 8, 128), F32),
            pltpu.VMEM((NX, TILES, 128), F32),
            pltpu.VMEM((4, 8, 128), F32),
            pltpu.VMEM((2, GROUP, 8, 128), F32),
            pltpu.VMEM((2, GROUP, SHARE, WIDTH), BF16),
            dma((NX + 1,)),
            dma((1,)), dma((1,)),
            dma((1,)), dma((1,)),
            dma((1,)), dma((NZ,)),
            dma((1,)), dma((NZ,)),
            dma((ITERS,)), dma((ITERS,)),
            dma((ITERS,)), dma((ITERS,)),
            dma((ITERS,)), dma((ITERS,)),
            dma((1,)), dma((1,)),
            dma((1,)), dma((1,)),
            dma((1,)), dma((1,)),
            dma((1,)), dma((1,)),
        ],
        compiler_params=pltpu.CompilerParams(
            collective_id=0, has_side_effects=True, vmem_limit_bytes=55172 * 1024),
        name="sinkhorn",
    )(noise_latents, teacher_latent_rows.T)
    row_pot, col_pot, targets = pl.pallas_call(
        give,
        out_shape=shapes,
        in_specs=[vmem, vmem, vmem],
        out_specs=(hbm, hbm, hbm),
        scratch_shapes=[dma((3,))],
        compiler_params=pltpu.CompilerParams(vmem_limit_bytes=2**20),
        name="give",
    )(*results)
    return row_pot.reshape(2048), col_pot.reshape(1024), targets


def solution(mesh):
    return jax.shard_map(
        shards,
        mesh=mesh,
        in_specs=(P(("noise", "sample"), None), P("sample", "noise")),
        out_specs=(P("noise"), P("sample"), P(("noise", "sample"), None)),
        check_vma=False,
    )
```

```python
import math

import jax
import jax.numpy as jnp
from jax import lax
from jax.experimental import pallas as pl
from jax.experimental.pallas import tpu as pltpu
from jax.sharding import PartitionSpec as P

ITERS = 3
WIDTH = 256
ROWS, COLS = 16384, 32768
STRENGTH = 0.1
NX, NY, NZ, NC = 4, 4, 8, 2
GROUP = NX * NY
SHARE = 64
BLOCK_ROWS = NZ * NC * SHARE
HALF = 512
FEATURES = WIDTH // (NX * NC)
PIECE = 256
PIECES = NY * HALF // PIECE
CUT = NC * SHARE
CUTS = NZ
TILES = PIECES * PIECE // 128
MESH = pl.DeviceIdType.MESH
F32, BF16 = jnp.float32, jnp.bfloat16
LN2 = math.log(2.0)
COST = 1.0 / (WIDTH * STRENGTH)


def spread(row):
    return jnp.broadcast_to(row, (128, 128)).T


def log2(a):
    return jnp.log(a) * (1.0 / LN2)


def lanes_of(t):
    return slice((t % 2) * 128, (t % 2) * 128 + 128)


def kernel(noise_hbm, teach_hbm, row_out, col_out, target_out, offer, cols, rows_x, tall, score, peak, total,
           gain, beta, plan, row_box, core_box, col_box, row_pot, col_pot, mine, gifts, boxes,
           load, s_offer, r_offer, s_x, s_y, r_x, r_y, s_xy, s_yx, r_xy, r_yx, s_rows, r_rows, s_pair, r_pair,
           s_row, r_row, s_core, r_core, s_col, r_col, s_rpot, r_rpot, s_cpot, r_cpot, s_gift, r_gift, s_box, r_box):
    n, s = lax.axis_index("noise"), lax.axis_index("sample")
    x, c = lax.div(n, NC), lax.rem(n, NC)
    y, z = lax.div(s, NZ), lax.rem(s, NZ)
    me = x * NY + y
    other = 1 - c
    xs = [x] + [lax.rem(x + d, NX) for d in range(1, NX)]
    ys = [y] + [lax.rem(y + d, NY) for d in range(1, NY)]
    zs = [z] + [lax.rem(z + d, NZ) for d in range(1, NZ)]
    noise_at = [px * NC + c for px in xs]
    across = [py * NZ + z for py in ys]
    along = [y * NZ + pz for pz in zs]
    sibling = (x * NC + other, s)
    xy = [(noise_at[k // NY], across[k % NY]) for k in range(1, GROUP)]
    ring = [1, 3, 2]
    near = [1, 7, 2, 6, 3, 5, 4]

    def send(src, dst, send_sem, recv_sem, device):
        pltpu.make_async_remote_copy(src_ref=src, dst_ref=dst, send_sem=send_sem, recv_sem=recv_sem,
                                     device_id=device, device_id_type=MESH).start()

    def wait(ref, sem):
        pltpu.make_async_copy(ref, ref, sem).wait()

    def half(which):
        return teach_hbm.at[:, pl.ds(pl.multiple_of(which * HALF, HALF), HALF)]

    own = cols.at[y, x, c]
    theirs = cols.at[y, x, other]
    loads = [pltpu.make_async_copy(half(other), offer, load.at[0]),
             pltpu.make_async_copy(half(c), own, load.at[1]),
             pltpu.make_async_copy(noise_hbm, rows_x.at[z, c], load.at[2])]
    for copy in loads:
        copy.start()

    barrier = pltpu.get_barrier_semaphore()
    greeted = xy + [(n, along[d]) for d in range(1, NZ)] + [sibling]
    for device in greeted:
        pl.semaphore_signal(barrier, inc=1, device_id=device, device_id_type=MESH)
    peak[...] = jnp.full((BLOCK_ROWS, 128), -1e30, F32)
    total[...] = jnp.zeros((BLOCK_ROWS, 128), F32)
    for copy in loads:
        copy.wait()
    pl.semaphore_wait(barrier, len(greeted))

    send(offer, cols.at[y, x, c], s_offer.at[0], r_offer.at[0], sibling)
    for d in ring:
        send(own, own, s_x.at[0], r_x.at[x], (noise_at[d], s))
        send(own, own, s_x.at[0], r_xy.at[y], (n, across[d]))
    for d in near:
        send(rows_x.at[z, c], rows_x.at[z, c], s_rows.at[0], r_rows.at[z], (n, along[d]))
    send(rows_x.at[z, c], rows_x.at[z, c], s_pair.at[0], r_pair.at[0], sibling)
    wait(theirs, r_offer.at[0])
    for d in ring:
        send(theirs, theirs, s_y.at[0], r_y.at[y], (n, across[d]))
        send(theirs, theirs, s_y.at[0], r_yx.at[y], (noise_at[d], s))
    for d in ring:
        passed = cols.at[y, xs[d], c]
        wait(passed, r_x.at[xs[d]])
        for e in ring:
            send(passed, passed, s_xy.at[0], r_xy.at[y], (n, across[e]))
        passed = cols.at[ys[d], x, other]
        wait(passed, r_y.at[ys[d]])
        for e in ring:
            send(passed, passed, s_yx.at[0], r_yx.at[ys[d]], (noise_at[e], s))
    for d in near:
        passed = rows_x.at[zs[d], c]
        wait(passed, r_rows.at[zs[d]])
        send(passed, passed, s_pair.at[0], r_pair.at[0], sibling)
    wait(rows_x.at[:, other], r_pair.at[0])

    def block_of(py, part):
        return cols[py, :, :, :, part * PIECE:(part + 1) * PIECE].reshape(WIDTH, PIECE)

    def scores_of(py, part):
        block = block_of(py, part)
        wide = block.astype(F32)
        norms = jnp.sum(wide * wide, axis=0, keepdims=True) * (COST / LN2)
        for b in range(CUTS):
            r = slice(b * CUT, (b + 1) * CUT)
            dots = jnp.dot(rows_x[b].reshape(CUT, WIDTH), block, preferred_element_type=F32)
            h = dots * (2.0 * COST / LN2) - norms
            score[py * 2 + part, r, :] = h
            left, right = h[:, :128], h[:, 128:]
            old = peak[r, :]
            new = jnp.maximum(old, jnp.maximum(left, right))
            total[r, :] = total[r, :] * jnp.exp2(old - new) + (jnp.exp2(left - new) + jnp.exp2(right - new))
            peak[r, :] = new

    def piece(k, carry):
        py = lax.rem(y + k, NY)

        @pl.when(k > 0)
        def _():
            wait(cols.at[py, :, c], r_xy.at[py])

        wait(cols.at[py, 0:NX - 1, other], r_yx.at[py])
        scores_of(py, 0)
        scores_of(py, 1)
        return carry

    lax.fori_loop(0, NY, piece, 0)

    def row_start(turn):
        for d in near:
            send(row_box.at[turn, z], row_box.at[turn, z], s_row.at[turn], r_row.at[turn], (n, along[d]))

    def row_wait(turn):
        wait(row_box.at[turn, 0:NZ - 1], r_row.at[turn])

    def core_trade(turn, value):
        core_box[turn, c] = value
        send(core_box.at[turn, c], core_box.at[turn, c], s_core.at[turn], r_core.at[turn], sibling)
        wait(core_box.at[turn, other], r_core.at[turn])
        return core_box[turn]

    def col_trade(turn):
        for device in xy:
            send(col_box.at[turn, me], col_box.at[turn, me], s_col.at[turn], r_col.at[turn], device)
        wait(col_box.at[turn, 0:GROUP - 1], r_col.at[turn])

    def log_sum(logs):
        top = jnp.max(logs, axis=0)
        return top + log2(jnp.sum(jnp.exp2(logs - top), axis=0))

    for b in range(CUTS):
        r = slice(b * CUT, (b + 1) * CUT)
        lane_peak = peak[r, :].T
        lane_total = total[r, :].T
        top = jnp.max(lane_peak, axis=0, keepdims=True)
        sums = jnp.sum(lane_total * jnp.exp2(lane_peak - top), axis=0, keepdims=True)
        row_box[0, z, b:b + 1, :] = top + log2(sums)
    row_start(0)
    for u in range(PIECES):
        tall[u * PIECE:(u + 1) * PIECE, :] = block_of(u // 2, u % 2).astype(F32).T.astype(BF16)
    for b in range(CUTS):
        latents = rows_x[b].reshape(CUT, WIDTH).astype(F32)
        squares = latents * latents
        mine[0, b:b + 1, :] = jnp.sum((squares[:, :128] + squares[:, 128:]).T, axis=0, keepdims=True)
    row_wait(0)
    row_log = -math.log2(ROWS) - log_sum(core_trade(0, log_sum(row_box[0])))

    mine[1] = row_log

    def first_column(b, carry):
        r = pl.ds(pl.multiple_of(b * CUT, CUT), CUT)
        shift = spread(mine[1, pl.ds(b, 1), :])
        for t in range(TILES):
            h = (score[t // 2, r, lanes_of(t)] + shift).reshape(CUT // 8, 8, 128)
            top = jnp.max(h, axis=0)
            e = jnp.exp2(h - top)
            score[t // 2, r, lanes_of(t)] = e.reshape(CUT, 128)
            gain[b, t] = top
            beta[b, t] = jnp.sum(e, axis=0)
        return carry

    lax.fori_loop(0, CUTS, first_column, 0)
    for t in range(TILES):
        cut_peak = gain[:, t]
        top = jnp.max(jnp.max(cut_peak, axis=0), axis=0, keepdims=True)
        sums = jnp.sum(jnp.sum(beta[:, t] * jnp.exp2(cut_peak - top), axis=0), axis=0, keepdims=True)
        col_box[0, me, t:t + 1, :] = top + log2(sums)
    col_trade(0)
    col_log = -math.log2(COLS) - log_sum(col_box[0])
    for t in range(TILES):
        start_gain = jnp.exp2(gain[:, t] + col_log[t:t + 1, :])
        gain[:, t] = start_gain
        beta[:, t] = start_gain

    alpha = None
    for turn in range(1, ITERS):
        for b in range(CUTS):
            r = slice(b * CUT, (b + 1) * CUT)
            acc = None
            for t in range(TILES):
                term = score[t // 2, r, lanes_of(t)].reshape(CUT // 8, 8, 128) * beta[b, t]
                acc = term if acc is None else acc + term
            row_box[turn, z, b:b + 1, :] = jnp.sum(acc.reshape(CUT, 128).T, axis=0, keepdims=True)
        row_start(turn)
        row_wait(turn)
        pair = core_trade(turn, jnp.sum(row_box[turn], axis=0))
        alpha = 1.0 / (ROWS * (pair[0] + pair[1]))

        sums = [None] * TILES
        for b in range(CUTS):
            r = slice(b * CUT, (b + 1) * CUT)
            weight = spread(alpha[b:b + 1, :])
            if turn == ITERS - 1:
                total[r, :] = weight
            for t in range(TILES):
                term = score[t // 2, r, lanes_of(t)] * weight
                term = jnp.sum(term.reshape(CUT // 8, 8, 128), axis=0) * gain[b, t]
                sums[t] = term if b == 0 else sums[t] + term
        for t in range(TILES):
            col_box[turn, me, t:t + 1, :] = jnp.sum(sums[t], axis=0, keepdims=True)
        col_trade(turn)
        factor = 1.0 / (COLS * jnp.sum(col_box[turn], axis=0))
        for t in range(TILES):
            beta[:, t] = gain[:, t] * factor[t:t + 1, :]

    order = [4, 3, 5, 2, 6, 7, 1, 0]

    def project(which, group):
        for k in range(4):
            pz = zs[order[4 * group + k]]
            r = pl.ds(pl.multiple_of(pz * CUT + which * SHARE, SHARE), SHARE)
            weight = total[r, :]
            acc = None
            for t in range(TILES):
                p = (score[t // 2, r, lanes_of(t)] * weight).reshape(SHARE // 8, 8, 128) * beta[pz, t]
                acc = p if acc is None else acc + p
                plan[k * SHARE:(k + 1) * SHARE, t * 128:t * 128 + 128] = p.reshape(SHARE, 128).astype(BF16)
            peak[r, :] = acc.reshape(SHARE, 128)
        return jnp.dot(plan[...], tall[...], preferred_element_type=F32)

    for group in range(2):
        gifts[0, group] = project(other, group).astype(BF16)
        send(gifts.at[0, group], gifts.at[1, group], s_gift.at[group], r_gift.at[group], sibling)
    for group in range(2):
        numer = project(c, group)
        wait(gifts.at[1, group], r_gift.at[group])
        numer = (numer + gifts[1, group].astype(F32)).astype(BF16)
        for k in range(4):
            d = order[4 * group + k]
            boxes[0, d] = numer[k * SHARE:(k + 1) * SHARE, :]
            if d:
                send(boxes.at[0, d], boxes.at[1, z], s_box.at[0], r_box.at[0], (n, along[d]))
    boxes[1, z] = boxes[0, 0]
    for b in range(CUTS):
        row_box[ITERS, z, b:b + 1, :] = jnp.sum(peak[b * CUT:(b + 1) * CUT, :].T, axis=0, keepdims=True)
    row_start(ITERS)

    row_pot[y] = COST * mine[0] + LN2 * (row_log + log2(alpha))
    col_pot[c] = LN2 * (col_log + log2(factor))
    for d in ring:
        send(row_pot.at[y], row_pot.at[y], s_rpot.at[0], r_rpot.at[0], (n, across[d]))
    send(col_pot.at[c], col_pot.at[c], s_cpot.at[0], r_cpot.at[0], sibling)
    wait(col_pot.at[other], r_cpot.at[0])
    for pc in range(NC):
        for q in range(HALF // 128):
            col_out[4 * pc + q:4 * pc + q + 1, :] = col_pot[pc, pl.ds(4 * y + q, 1), :]
    wait(row_pot.at[0:NY - 1], r_rpot.at[0])
    low = lax.broadcasted_iota(jnp.int32, (NZ // 2, 128), 1) < SHARE
    for py in range(NY):
        pairs = row_pot[py].reshape(NZ // 2, 2, 128)
        even, odd = pairs[:, 0], pairs[:, 1]
        even_low = jnp.where(c == 0, even, pltpu.roll(even, SHARE, 1))
        odd_high = jnp.where(c == 0, pltpu.roll(odd, SHARE, 1), odd)
        row_out[4 * py:4 * py + 4, :] = jnp.where(low, even_low, odd_high)

    row_wait(ITERS)
    pair = core_trade(ITERS, jnp.sum(row_box[ITERS], axis=0))
    mine[1] = pair[0] + pair[1]
    total[0:128, :] = spread(mine[1, pl.ds(z, 1), :])
    mass = total[pl.ds(pl.multiple_of(c * SHARE, SHARE), SHARE), :]
    wait(boxes.at[1, 0:NZ - 1], r_box.at[0])
    numer = jnp.sum(boxes[1].astype(F32), axis=0)
    target_out[:, :128] = (numer[:, :128] / mass).astype(BF16)
    target_out[:, 128:] = (numer[:, 128:] / mass).astype(BF16)

    wait(offer, s_offer.at[0])
    wait(cols.at[0, 0:3], s_x.at[0])
    wait(cols.at[0, 0:3], s_y.at[0])
    wait(cols.at[0:3, 0:3, 0], s_xy.at[0])
    wait(cols.at[0:3, 0:3, 0], s_yx.at[0])
    wait(rows_x.at[0:NZ - 1, 0], s_rows.at[0])
    wait(rows_x.at[:, 0], s_pair.at[0])
    for turn in range(ITERS + 1):
        wait(row_box.at[turn, 0:NZ - 1], s_row.at[turn])
        wait(core_box.at[turn, c], s_core.at[turn])
    for turn in range(ITERS):
        wait(col_box.at[turn, 0:GROUP - 1], s_col.at[turn])
    wait(row_pot.at[0:NY - 1], s_rpot.at[0])
    wait(col_pot.at[c], s_cpot.at[0])
    for group in range(2):
        wait(gifts.at[0, group], s_gift.at[group])
    wait(boxes.at[1, 0:NZ - 1], s_box.at[0])


def give(a, b, c, a_out, b_out, c_out, sems):
    copies = [pltpu.make_async_copy(src, dst, sems.at[k])
              for k, (src, dst) in enumerate(((a, a_out), (b, b_out), (c, c_out)))]
    for copy in copies:
        copy.start()
    for copy in copies:
        copy.wait()


def shards(noise_latents, teacher_latent_rows):
    vmem = pl.BlockSpec(memory_space=pltpu.VMEM)
    hbm = pl.BlockSpec(memory_space=pltpu.HBM)
    dma = pltpu.SemaphoreType.DMA
    shapes = (
        jax.ShapeDtypeStruct((16, 128), F32),
        jax.ShapeDtypeStruct((8, 128), F32),
        jax.ShapeDtypeStruct((SHARE, WIDTH), BF16),
    )
    results = pl.pallas_call(
        kernel,
        out_shape=shapes,
        in_specs=[hbm, hbm],
        out_specs=(vmem, vmem, vmem),
        scratch_shapes=[
            pltpu.VMEM((FEATURES, HALF), BF16),
            pltpu.VMEM((NY, NX, NC, FEATURES, HALF), BF16),
            pltpu.VMEM((NZ, NC, SHARE, WIDTH), BF16),
            pltpu.VMEM((PIECES * PIECE, WIDTH), BF16),
            pltpu.VMEM((PIECES, BLOCK_ROWS, PIECE), F32),
            pltpu.VMEM((BLOCK_ROWS, 128), F32),
            pltpu.VMEM((BLOCK_ROWS, 128), F32),
            pltpu.VMEM((CUTS, TILES, 8, 128), F32),
            pltpu.VMEM((CUTS, TILES, 8, 128), F32),
            pltpu.VMEM((4 * SHARE, PIECES * PIECE), BF16),
            pltpu.VMEM((ITERS + 1, NZ, 8, 128), F32),
            pltpu.VMEM((ITERS + 1, NC, 8, 128), F32),
            pltpu.VMEM((ITERS, GROUP, TILES, 128), F32),
            pltpu.VMEM((NY, 8, 128), F32),
            pltpu.VMEM((NC, TILES, 128), F32),
            pltpu.VMEM((2, 8, 128), F32),
            pltpu.VMEM((2, 2, 4 * SHARE, WIDTH), BF16),
            pltpu.VMEM((2, NZ, SHARE, WIDTH), BF16),
            dma((3,)),
            dma((1,)), dma((1,)),
            dma((1,)), dma((1,)), dma((NX,)), dma((NY,)),
            dma((1,)), dma((1,)), dma((NY,)), dma((NY,)),
            dma((1,)), dma((NZ,)),
            dma((1,)), dma((1,)),
            dma((ITERS + 1,)), dma((ITERS + 1,)),
            dma((ITERS + 1,)), dma((ITERS + 1,)),
            dma((ITERS,)), dma((ITERS,)),
            dma((1,)), dma((1,)),
            dma((1,)), dma((1,)),
            dma((2,)), dma((2,)),
            dma((1,)), dma((1,)),
        ],
        compiler_params=pltpu.CompilerParams(
            collective_id=0, has_side_effects=True, vmem_limit_bytes=55172 * 1024),
        name="sinkhorn",
    )(noise_latents, teacher_latent_rows.T)
    row_pot, col_pot, targets = pl.pallas_call(
        give,
        out_shape=shapes,
        in_specs=[vmem, vmem, vmem],
        out_specs=(hbm, hbm, hbm),
        scratch_shapes=[dma((3,))],
        compiler_params=pltpu.CompilerParams(vmem_limit_bytes=2**20),
        name="give",
    )(*results)
    return row_pot.reshape(2048), col_pot.reshape(1024), targets


def solution(mesh):
    return jax.shard_map(
        shards,
        mesh=mesh,
        in_specs=(P(("noise", "sample"), None), P("sample", "noise")),
        out_specs=(P("noise"), P("sample"), P(("noise", "sample"), None)),
        check_vma=False,
    )
```

```python
import math

import jax
import jax.numpy as jnp
from jax import lax
from jax.experimental import pallas as pl
from jax.experimental.pallas import tpu as pltpu
from jax.sharding import PartitionSpec as P

ITERS = 3
WIDTH = 256
ROWS, COLS = 16384, 32768
STRENGTH = 0.1
NX, NY, NZ, NC = 4, 4, 8, 2
GROUP = NX * NY
SHARE = 64
BLOCK_ROWS = NZ * NC * SHARE
HALF = 512
FEATURES = WIDTH // (NX * NC)
PIECE = 256
PIECES = NY * HALF // PIECE
CUT = NC * SHARE
CUTS = NZ
TILES = PIECES * PIECE // 128
MESH = pl.DeviceIdType.MESH
F32, BF16 = jnp.float32, jnp.bfloat16
LN2 = math.log(2.0)
COST = 1.0 / (WIDTH * STRENGTH)


def spread(row):
    return jnp.broadcast_to(row, (128, 128)).T


def log2(a):
    return jnp.log(a) * (1.0 / LN2)


def lanes_of(t):
    return slice((t % 2) * 128, (t % 2) * 128 + 128)


def kernel(noise_hbm, teach_hbm, row_out, col_out, target_out, offer, cols, rows_x, tall, score, peak, total,
           gain, beta, plan, row_box, core_box, col_box, sum_box, row_pot, col_pot, mine, gifts, boxes,
           load, s_offer, r_offer, s_x, s_y, r_x, r_y, s_xy, s_yx, r_xy, r_yx, s_rows, r_rows, s_pair, r_pair,
           s_row, r_row, s_core, r_core, s_col, r_col, s_rpot, r_rpot, s_cpot, r_cpot, s_gift, r_gift, s_box, r_box):
    n, s = lax.axis_index("noise"), lax.axis_index("sample")
    x, c = lax.div(n, NC), lax.rem(n, NC)
    y, z = lax.div(s, NZ), lax.rem(s, NZ)
    me = x * NY + y
    other = 1 - c
    xs = [x] + [lax.rem(x + d, NX) for d in range(1, NX)]
    ys = [y] + [lax.rem(y + d, NY) for d in range(1, NY)]
    zs = [z] + [lax.rem(z + d, NZ) for d in range(1, NZ)]
    noise_at = [px * NC + c for px in xs]
    across = [py * NZ + z for py in ys]
    along = [y * NZ + pz for pz in zs]
    sibling = (x * NC + other, s)
    xy = [(noise_at[k // NY], across[k % NY]) for k in range(1, GROUP)]
    ring = [1, 3, 2]
    near = [1, 7, 2, 6, 3, 5, 4]

    def send(src, dst, send_sem, recv_sem, device):
        pltpu.make_async_remote_copy(src_ref=src, dst_ref=dst, send_sem=send_sem, recv_sem=recv_sem,
                                     device_id=device, device_id_type=MESH).start()

    def wait(ref, sem):
        pltpu.make_async_copy(ref, ref, sem).wait()

    def half(which):
        return teach_hbm.at[:, pl.ds(pl.multiple_of(which * HALF, HALF), HALF)]

    own = cols.at[y, x, c]
    theirs = cols.at[y, x, other]
    loads = [pltpu.make_async_copy(half(other), offer, load.at[0]),
             pltpu.make_async_copy(half(c), own, load.at[1]),
             pltpu.make_async_copy(noise_hbm, rows_x.at[z, c], load.at[2])]
    for copy in loads:
        copy.start()

    barrier = pltpu.get_barrier_semaphore()
    greeted = xy + [(n, along[d]) for d in range(1, NZ)] + [sibling]
    for device in greeted:
        pl.semaphore_signal(barrier, inc=1, device_id=device, device_id_type=MESH)
    peak[...] = jnp.full((BLOCK_ROWS, 128), -1e30, F32)
    total[...] = jnp.zeros((BLOCK_ROWS, 128), F32)
    for copy in loads:
        copy.wait()
    pl.semaphore_wait(barrier, len(greeted))

    send(offer, cols.at[y, x, c], s_offer.at[0], r_offer.at[0], sibling)
    for d in ring:
        send(own, own, s_x.at[0], r_x.at[x], (noise_at[d], s))
        send(own, own, s_x.at[0], r_xy.at[y], (n, across[d]))
    for d in near:
        send(rows_x.at[z, c], rows_x.at[z, c], s_rows.at[0], r_rows.at[z], (n, along[d]))
    send(rows_x.at[z, c], rows_x.at[z, c], s_pair.at[0], r_pair.at[0], sibling)
    wait(theirs, r_offer.at[0])
    for d in ring:
        send(theirs, theirs, s_y.at[0], r_y.at[y], (n, across[d]))
        send(theirs, theirs, s_y.at[0], r_yx.at[y], (noise_at[d], s))
    for d in ring:
        wait(cols.at[y, xs[d], c], r_x.at[xs[d]])
    for q in (3, 1, 2):
        for d in ring:
            passed = cols.at[y, xs[d], c]
            send(passed, passed, s_xy.at[0], r_xy.at[y], (n, across[NY - q]))
        passed = cols.at[ys[q], x, other]
        wait(passed, r_y.at[ys[q]])
        for e in ring:
            send(passed, passed, s_yx.at[0], r_yx.at[ys[q]], (noise_at[e], s))
    for d in near:
        passed = rows_x.at[zs[d], c]
        wait(passed, r_rows.at[zs[d]])
        send(passed, passed, s_pair.at[0], r_pair.at[0], sibling)
    wait(rows_x.at[:, other], r_pair.at[0])

    def block_of(py, part):
        return cols[py, :, :, :, part * PIECE:(part + 1) * PIECE].reshape(WIDTH, PIECE)

    def scores_of(py, part):
        block = block_of(py, part)
        wide = block.astype(F32)
        norms = jnp.sum(wide * wide, axis=0, keepdims=True) * (COST / LN2)
        for b in range(CUTS):
            r = slice(b * CUT, (b + 1) * CUT)
            dots = jnp.dot(rows_x[b].reshape(CUT, WIDTH), block, preferred_element_type=F32)
            h = dots * (2.0 * COST / LN2) - norms
            score[py * 2 + part, r, :] = h
            left, right = h[:, :128], h[:, 128:]
            old = peak[r, :]
            new = jnp.maximum(old, jnp.maximum(left, right))
            total[r, :] = total[r, :] * jnp.exp2(old - new) + (jnp.exp2(left - new) + jnp.exp2(right - new))
            peak[r, :] = new

    def piece(k, carry):
        py = lax.rem(y + lax.div(3 * k * (k + 1), 2), NY)

        @pl.when(k > 0)
        def _():
            wait(cols.at[py, :, c], r_xy.at[py])

        wait(cols.at[py, 0:NX - 1, other], r_yx.at[py])
        scores_of(py, 0)
        scores_of(py, 1)
        return carry

    lax.fori_loop(0, NY, piece, 0)

    def row_start(turn):
        for d in near:
            send(row_box.at[turn, z], row_box.at[turn, z], s_row.at[turn], r_row.at[turn], (n, along[d]))

    def row_wait(turn):
        wait(row_box.at[turn, 0:NZ - 1], r_row.at[turn])

    def core_trade(turn, value):
        core_box[turn, c] = value
        send(core_box.at[turn, c], core_box.at[turn, c], s_core.at[turn], r_core.at[turn], sibling)
        wait(core_box.at[turn, other], r_core.at[turn])
        return core_box[turn]

    def col_trade(turn):
        box = col_box if turn == 0 else sum_box.at[turn - 1]
        for device in xy:
            send(box.at[me], box.at[me], s_col.at[turn], r_col.at[turn], device)
        wait(box.at[0:GROUP - 1], r_col.at[turn])

    def log_sum(logs):
        top = jnp.max(logs, axis=0)
        return top + log2(jnp.sum(jnp.exp2(logs - top), axis=0))

    for b in range(CUTS):
        r = slice(b * CUT, (b + 1) * CUT)
        lane_peak = peak[r, :].T
        lane_total = total[r, :].T
        top = jnp.max(lane_peak, axis=0, keepdims=True)
        sums = jnp.sum(lane_total * jnp.exp2(lane_peak - top), axis=0, keepdims=True)
        row_box[0, z, b:b + 1, :] = top + log2(sums)
    row_start(0)
    for u in range(PIECES):
        tall[u * PIECE:(u + 1) * PIECE, :] = block_of(u // 2, u % 2).astype(F32).T.astype(BF16)
    for b in range(CUTS):
        latents = rows_x[b].reshape(CUT, WIDTH).astype(F32)
        squares = latents * latents
        mine[0, b:b + 1, :] = jnp.sum((squares[:, :128] + squares[:, 128:]).T, axis=0, keepdims=True)
    row_wait(0)
    row_log = -math.log2(ROWS) - log_sum(core_trade(0, log_sum(row_box[0])))

    mine[1] = row_log

    def first_column(b, carry):
        r = slice(b * CUT, (b + 1) * CUT)
        shift = spread(row_log[b:b + 1, :])
        for t in range(TILES):
            h = (score[t // 2, r, lanes_of(t)] + shift).reshape(CUT // 8, 8, 128)
            top = jnp.max(h, axis=0)
            e = jnp.exp2(h - top)
            score[t // 2, r, lanes_of(t)] = e.reshape(CUT, 128)
            gain[b, t] = top
            beta[b, t] = jnp.sum(e, axis=0)
        return carry

    for b in range(CUTS):
        first_column(b, 0)
    for t in range(TILES):
        cut_peak = gain[:, t]
        top = jnp.max(jnp.max(cut_peak, axis=0), axis=0, keepdims=True)
        sums = jnp.sum(jnp.sum(beta[:, t] * jnp.exp2(cut_peak - top), axis=0), axis=0, keepdims=True)
        col_box[me, t:t + 1, :] = top + log2(sums)
    col_trade(0)
    col_log = -math.log2(COLS) - log_sum(col_box[...])
    for t in range(TILES):
        start_gain = jnp.exp2(gain[:, t] + col_log[t:t + 1, :])
        gain[:, t] = start_gain
        beta[:, t] = start_gain

    alpha = None
    for turn in range(1, ITERS):
        for b in range(CUTS):
            r = slice(b * CUT, (b + 1) * CUT)
            acc = None
            for t in range(TILES):
                term = score[t // 2, r, lanes_of(t)].reshape(CUT // 8, 8, 128) * beta[b, t]
                acc = term if acc is None else acc + term
            row_box[turn, z, b:b + 1, :] = jnp.sum(acc.reshape(CUT, 128).T, axis=0, keepdims=True)
        row_start(turn)
        row_wait(turn)
        pair = core_trade(turn, jnp.sum(row_box[turn], axis=0))
        alpha = 1.0 / (ROWS * (pair[0] + pair[1]))

        sums = [None] * TILES
        for b in range(CUTS):
            r = slice(b * CUT, (b + 1) * CUT)
            weight = spread(alpha[b:b + 1, :])
            if turn == ITERS - 1:
                total[r, :] = weight
            for t in range(TILES):
                term = score[t // 2, r, lanes_of(t)] * weight
                term = jnp.sum(term.reshape(CUT // 8, 8, 128), axis=0) * gain[b, t]
                sums[t] = term if b == 0 else sums[t] + term
        sums = [jnp.sum(part, axis=0, keepdims=True) for part in sums]
        sum_box[turn - 1, me] = jnp.concatenate(sums, axis=0).astype(BF16)
        col_trade(turn)
        factor = 1.0 / (COLS * jnp.sum(sum_box[turn - 1].astype(F32), axis=0))
        for t in range(TILES):
            beta[:, t] = gain[:, t] * factor[t:t + 1, :]

    order = [4, 3, 5, 2, 6, 7, 1, 0]

    def project(which, group):
        for k in range(4):
            pz = zs[order[4 * group + k]]
            r = pl.ds(pl.multiple_of(pz * CUT + which * SHARE, SHARE), SHARE)
            weight = total[r, :]
            acc = None
            for t in range(TILES):
                p = (score[t // 2, r, lanes_of(t)] * weight).reshape(SHARE // 8, 8, 128) * beta[pz, t]
                acc = p if acc is None else acc + p
                plan[k * SHARE:(k + 1) * SHARE, t * 128:t * 128 + 128] = p.reshape(SHARE, 128).astype(BF16)
            peak[r, :] = acc.reshape(SHARE, 128)
        return jnp.dot(plan[...], tall[...], preferred_element_type=F32)

    for group in range(2):
        gifts[0, group] = project(other, group).astype(BF16)
        send(gifts.at[0, group], gifts.at[1, group], s_gift.at[group], r_gift.at[group], sibling)
    for group in range(2):
        numer = project(c, group)
        wait(gifts.at[1, group], r_gift.at[group])
        numer = (numer + gifts[1, group].astype(F32)).astype(BF16)
        for k in range(4):
            d = order[4 * group + k]
            boxes[0, d] = numer[k * SHARE:(k + 1) * SHARE, :]
            if d:
                send(boxes.at[0, d], boxes.at[1, z], s_box.at[0], r_box.at[0], (n, along[d]))
    boxes[1, z] = boxes[0, 0]
    for b in range(CUTS):
        row_box[ITERS, z, b:b + 1, :] = jnp.sum(peak[b * CUT:(b + 1) * CUT, :].T, axis=0, keepdims=True)
    row_start(ITERS)

    row_pot[y] = COST * mine[0] + LN2 * (row_log + log2(alpha))
    col_pot[c] = LN2 * (col_log + log2(factor))
    for d in ring:
        send(row_pot.at[y], row_pot.at[y], s_rpot.at[0], r_rpot.at[0], (n, across[d]))
    send(col_pot.at[c], col_pot.at[c], s_cpot.at[0], r_cpot.at[0], sibling)
    wait(col_pot.at[other], r_cpot.at[0])
    for pc in range(NC):
        for q in range(HALF // 128):
            col_out[4 * pc + q:4 * pc + q + 1, :] = col_pot[pc, pl.ds(4 * y + q, 1), :]
    wait(row_pot.at[0:NY - 1], r_rpot.at[0])
    low = lax.broadcasted_iota(jnp.int32, (NZ // 2, 128), 1) < SHARE
    for py in range(NY):
        pairs = row_pot[py].reshape(NZ // 2, 2, 128)
        even, odd = pairs[:, 0], pairs[:, 1]
        even_low = jnp.where(c == 0, even, pltpu.roll(even, SHARE, 1))
        odd_high = jnp.where(c == 0, pltpu.roll(odd, SHARE, 1), odd)
        row_out[4 * py:4 * py + 4, :] = jnp.where(low, even_low, odd_high)

    row_wait(ITERS)
    pair = core_trade(ITERS, jnp.sum(row_box[ITERS], axis=0))
    mine[1] = pair[0] + pair[1]
    total[0:128, :] = spread(mine[1, pl.ds(z, 1), :])
    mass = total[pl.ds(pl.multiple_of(c * SHARE, SHARE), SHARE), :]
    wait(boxes.at[1, 0:NZ - 1], r_box.at[0])
    numer = jnp.sum(boxes[1].astype(F32), axis=0)
    target_out[:, :128] = (numer[:, :128] / mass).astype(BF16)
    target_out[:, 128:] = (numer[:, 128:] / mass).astype(BF16)

    wait(offer, s_offer.at[0])
    wait(cols.at[0, 0:3], s_x.at[0])
    wait(cols.at[0, 0:3], s_y.at[0])
    wait(cols.at[0:3, 0:3, 0], s_xy.at[0])
    wait(cols.at[0:3, 0:3, 0], s_yx.at[0])
    wait(rows_x.at[0:NZ - 1, 0], s_rows.at[0])
    wait(rows_x.at[:, 0], s_pair.at[0])
    for turn in range(ITERS + 1):
        wait(row_box.at[turn, 0:NZ - 1], s_row.at[turn])
        wait(core_box.at[turn, c], s_core.at[turn])
    for turn in range(ITERS):
        wait((col_box if turn == 0 else sum_box.at[turn - 1]).at[0:GROUP - 1], s_col.at[turn])
    wait(row_pot.at[0:NY - 1], s_rpot.at[0])
    wait(col_pot.at[c], s_cpot.at[0])
    for group in range(2):
        wait(gifts.at[0, group], s_gift.at[group])
    wait(boxes.at[1, 0:NZ - 1], s_box.at[0])


def give(a, b, c, a_out, b_out, c_out, sems):
    copies = [pltpu.make_async_copy(src, dst, sems.at[k])
              for k, (src, dst) in enumerate(((a, a_out), (b, b_out), (c, c_out)))]
    for copy in copies:
        copy.start()
    for copy in copies:
        copy.wait()


def shards(noise_latents, teacher_latent_rows):
    vmem = pl.BlockSpec(memory_space=pltpu.VMEM)
    hbm = pl.BlockSpec(memory_space=pltpu.HBM)
    dma = pltpu.SemaphoreType.DMA
    shapes = (
        jax.ShapeDtypeStruct((16, 128), F32),
        jax.ShapeDtypeStruct((8, 128), F32),
        jax.ShapeDtypeStruct((SHARE, WIDTH), BF16),
    )
    results = pl.pallas_call(
        kernel,
        out_shape=shapes,
        in_specs=[hbm, hbm],
        out_specs=(vmem, vmem, vmem),
        scratch_shapes=[
            pltpu.VMEM((FEATURES, HALF), BF16),
            pltpu.VMEM((NY, NX, NC, FEATURES, HALF), BF16),
            pltpu.VMEM((NZ, NC, SHARE, WIDTH), BF16),
            pltpu.VMEM((PIECES * PIECE, WIDTH), BF16),
            pltpu.VMEM((PIECES, BLOCK_ROWS, PIECE), F32),
            pltpu.VMEM((BLOCK_ROWS, 128), F32),
            pltpu.VMEM((BLOCK_ROWS, 128), F32),
            pltpu.VMEM((CUTS, TILES, 8, 128), F32),
            pltpu.VMEM((CUTS, TILES, 8, 128), F32),
            pltpu.VMEM((4 * SHARE, PIECES * PIECE), BF16),
            pltpu.VMEM((ITERS + 1, NZ, 8, 128), F32),
            pltpu.VMEM((ITERS + 1, NC, 8, 128), F32),
            pltpu.VMEM((GROUP, TILES, 128), F32),
            pltpu.VMEM((ITERS - 1, GROUP, TILES, 128), BF16),
            pltpu.VMEM((NY, 8, 128), F32),
            pltpu.VMEM((NC, TILES, 128), F32),
            pltpu.VMEM((2, 8, 128), F32),
            pltpu.VMEM((2, 2, 4 * SHARE, WIDTH), BF16),
            pltpu.VMEM((2, NZ, SHARE, WIDTH), BF16),
            dma((3,)),
            dma((1,)), dma((1,)),
            dma((1,)), dma((1,)), dma((NX,)), dma((NY,)),
            dma((1,)), dma((1,)), dma((NY,)), dma((NY,)),
            dma((1,)), dma((NZ,)),
            dma((1,)), dma((1,)),
            dma((ITERS + 1,)), dma((ITERS + 1,)),
            dma((ITERS + 1,)), dma((ITERS + 1,)),
            dma((ITERS,)), dma((ITERS,)),
            dma((1,)), dma((1,)),
            dma((1,)), dma((1,)),
            dma((2,)), dma((2,)),
            dma((1,)), dma((1,)),
        ],
        compiler_params=pltpu.CompilerParams(
            collective_id=0, has_side_effects=True, vmem_limit_bytes=55172 * 1024),
        name="sinkhorn",
    )(noise_latents, teacher_latent_rows.T)
    row_pot, col_pot, targets = pl.pallas_call(
        give,
        out_shape=shapes,
        in_specs=[vmem, vmem, vmem],
        out_specs=(hbm, hbm, hbm),
        scratch_shapes=[dma((3,))],
        compiler_params=pltpu.CompilerParams(vmem_limit_bytes=2**20),
        name="give",
    )(*results)
    return row_pot.reshape(2048), col_pot.reshape(1024), targets


def solution(mesh):
    return jax.shard_map(
        shards,
        mesh=mesh,
        in_specs=(P(("noise", "sample"), None), P("sample", "noise")),
        out_specs=(P("noise"), P("sample"), P(("noise", "sample"), None)),
        check_vma=False,
    )
```

```python
import math

import jax
import jax.numpy as jnp
from jax import lax
from jax.experimental import pallas as pl
from jax.experimental.pallas import tpu as pltpu
from jax.sharding import PartitionSpec as P

ITERS = 3
WIDTH = 256
ROWS, COLS = 16384, 32768
STRENGTH = 0.1
NX, NY, NZ, NC = 4, 4, 8, 2
GROUP = NX * NY
SHARE = 64
BLOCK_ROWS = NZ * NC * SHARE
HALF = 512
FEATURES = WIDTH // (NX * NC)
PIECE = 256
PIECES = NY * HALF // PIECE
CUT = NC * SHARE
CUTS = NZ
TILES = PIECES * PIECE // 128
MESH = pl.DeviceIdType.MESH
F32, BF16 = jnp.float32, jnp.bfloat16
LN2 = math.log(2.0)
COST = 1.0 / (WIDTH * STRENGTH)


def spread(row):
    return jnp.broadcast_to(row, (128, 128)).T


def log2(a):
    return jnp.log(a) * (1.0 / LN2)


def lanes_of(t):
    return slice((t % 2) * 128, (t % 2) * 128 + 128)


def kernel(noise_hbm, teach_hbm, row_out, col_out, target_out, offer, cols, rows_x, norms, tall, score, peak, total,
           gain, beta, plan, row_box, core_box, col_box, sum_box, row_pot, col_pot, mine, gifts, boxes,
           load, s_offer, r_offer, s_x, s_y, r_x, r_y, s_xy, s_yx, r_xy, r_yx, s_rows, r_rows, s_pair, r_pair,
           s_row, r_row, s_core, r_core, s_col, r_col, s_rpot, r_rpot, s_cpot, r_cpot, s_gift, r_gift, s_box, r_box):
    n, s = lax.axis_index("noise"), lax.axis_index("sample")
    x, c = lax.div(n, NC), lax.rem(n, NC)
    y, z = lax.div(s, NZ), lax.rem(s, NZ)
    me = x * NY + y
    other = 1 - c
    xs = [x] + [lax.rem(x + d, NX) for d in range(1, NX)]
    ys = [y] + [lax.rem(y + d, NY) for d in range(1, NY)]
    zs = [z] + [lax.rem(z + d, NZ) for d in range(1, NZ)]
    noise_at = [px * NC + c for px in xs]
    across = [py * NZ + z for py in ys]
    along = [y * NZ + pz for pz in zs]
    sibling = (x * NC + other, s)
    ring = [1, 3, 2]
    near = [1, 7, 2, 6, 3, 5, 4]
    far = near[::-1]
    corner = sorted(range(1, GROUP), key=lambda k: -(min(k // NY, NX - k // NY) + min(k % NY, NY - k % NY)))
    xy = [(noise_at[k // NY], across[k % NY]) for k in corner]

    def send(src, dst, send_sem, recv_sem, device):
        pltpu.make_async_remote_copy(src_ref=src, dst_ref=dst, send_sem=send_sem, recv_sem=recv_sem,
                                     device_id=device, device_id_type=MESH).start()

    def wait(ref, sem):
        pltpu.make_async_copy(ref, ref, sem).wait()

    def half(which):
        return teach_hbm.at[:, pl.ds(pl.multiple_of(which * HALF, HALF), HALF)]

    own = cols.at[y, x, c]
    theirs = cols.at[y, x, other]
    loads = [pltpu.make_async_copy(half(other), offer, load.at[0]),
             pltpu.make_async_copy(half(c), own, load.at[1]),
             pltpu.make_async_copy(noise_hbm, rows_x.at[z, c], load.at[2])]
    for copy in loads:
        copy.start()

    barrier = pltpu.get_barrier_semaphore()
    greeted = xy + [(n, along[d]) for d in range(1, NZ)] + [sibling]
    for device in greeted:
        pl.semaphore_signal(barrier, inc=1, device_id=device, device_id_type=MESH)
    peak[...] = jnp.full((BLOCK_ROWS, 128), -1e30, F32)
    total[...] = jnp.zeros((BLOCK_ROWS, 128), F32)
    for copy in loads:
        copy.wait()
    pl.semaphore_wait(barrier, len(greeted))

    send(offer, cols.at[y, x, c], s_offer.at[0], r_offer.at[0], sibling)
    for d in ring:
        send(own, own, s_x.at[0], r_x.at[x], (noise_at[d], s))
        send(own, own, s_x.at[0], r_xy.at[y], (n, across[d]))
    for d in near:
        send(rows_x.at[z, c], rows_x.at[z, c], s_rows.at[0], r_rows.at[z], (n, along[d]))
    send(rows_x.at[z, c], rows_x.at[z, c], s_pair.at[0], r_pair.at[z], sibling)
    wait(theirs, r_offer.at[0])
    for d in ring:
        send(theirs, theirs, s_y.at[0], r_y.at[y], (n, across[d]))
        send(theirs, theirs, s_y.at[0], r_yx.at[y], (noise_at[d], s))
    for d in ring:
        wait(cols.at[y, xs[d], c], r_x.at[xs[d]])
    for q in (3, 1, 2):
        for d in ring:
            passed = cols.at[y, xs[d], c]
            send(passed, passed, s_xy.at[0], r_xy.at[y], (n, across[NY - q]))
        passed = cols.at[ys[q], x, other]
        wait(passed, r_y.at[ys[q]])
        for e in ring:
            send(passed, passed, s_yx.at[0], r_yx.at[ys[q]], (noise_at[e], s))
    def block_of(py, part):
        return cols[py, :, :, :, part * PIECE:(part + 1) * PIECE].reshape(WIDTH, PIECE)

    def norms_of(py):
        for part in range(2):
            wide = block_of(py, part).astype(F32)
            norms[py * 2 + part] = jnp.sum(wide * wide, axis=0, keepdims=True) * (COST / LN2)

    def scores_of(py, blocks):
        for b in blocks:
            r = slice(b * CUT, (b + 1) * CUT) if isinstance(b, int) else pl.ds(pl.multiple_of(b * CUT, CUT), CUT)
            latents = rows_x[b].reshape(CUT, WIDTH)
            tiles = []
            for part in range(2):
                dots = jnp.dot(latents, block_of(py, part), preferred_element_type=F32)
                h = dots * (2.0 * COST / LN2) - norms[py * 2 + part]
                score[py * 2 + part, r, :] = h
                tiles += [h[:, :128], h[:, 128:]]
            old = peak[r, :]
            new = jnp.maximum(jnp.maximum(tiles[0], tiles[1]), jnp.maximum(tiles[2], tiles[3]))
            new = jnp.maximum(old, new)
            sums = [jnp.exp2(tile - new) for tile in tiles]
            total[r, :] = total[r, :] * jnp.exp2(old - new) + ((sums[0] + sums[1]) + (sums[2] + sums[3]))
            peak[r, :] = new

    def piece_wait(py):
        wait(cols.at[py, :, c], r_xy.at[py])
        wait(cols.at[py, 0:NX - 1, other], r_yx.at[py])
        norms_of(py)

    def off(k):
        return lax.rem(z + lax.div(k + 1, 2) * (2 * lax.rem(k, 2) - 1) + NZ, NZ)

    wait(cols.at[y, 0:NX - 1, other], r_yx.at[y])
    norms_of(y)

    def rows_in(k, carry):
        pz, last = off(k), off(k - 1)
        passed = rows_x.at[pz, c]
        wait(passed, r_rows.at[pz])
        send(passed, passed, s_pair.at[0], r_pair.at[pz], sibling)
        wait(rows_x.at[last, other], r_pair.at[last])
        scores_of(y, [last])
        return carry

    lax.fori_loop(1, NZ, rows_in, 0)
    wait(rows_x.at[zs[4], other], r_pair.at[zs[4]])
    scores_of(y, [zs[4]])

    def piece(k, carry):
        py = lax.rem(y + lax.div(3 * k * (k + 1), 2), NY)
        piece_wait(py)
        scores_of(py, range(CUTS))
        return carry

    lax.fori_loop(1, NY, piece, 0)

    def row_start(turn):
        for d in far:
            send(row_box.at[turn, z], row_box.at[turn, z], s_row.at[turn], r_row.at[turn], (n, along[d]))

    def row_wait(turn):
        wait(row_box.at[turn, 0:NZ - 1], r_row.at[turn])

    def core_trade(turn, value):
        core_box[turn, c] = value
        send(core_box.at[turn, c], core_box.at[turn, c], s_core.at[turn], r_core.at[turn], sibling)
        wait(core_box.at[turn, other], r_core.at[turn])
        return core_box[turn]

    def col_trade(turn):
        box = col_box if turn == 0 else sum_box.at[turn - 1]
        for device in xy:
            send(box.at[me], box.at[me], s_col.at[turn], r_col.at[turn], device)
        wait(box.at[0:GROUP - 1], r_col.at[turn])

    def log_sum(logs):
        top = jnp.max(logs, axis=0)
        return top + log2(jnp.sum(jnp.exp2(logs - top), axis=0))

    for b in range(CUTS):
        r = slice(b * CUT, (b + 1) * CUT)
        lane_peak = peak[r, :].T
        lane_total = total[r, :].T
        top = jnp.max(lane_peak, axis=0, keepdims=True)
        sums = jnp.sum(lane_total * jnp.exp2(lane_peak - top), axis=0, keepdims=True)
        row_box[0, z, b:b + 1, :] = top + log2(sums)
    row_start(0)
    for u in range(PIECES):
        tall[u * PIECE:(u + 1) * PIECE, :] = block_of(u // 2, u % 2).astype(F32).T.astype(BF16)
    for b in range(CUTS):
        latents = rows_x[b].reshape(CUT, WIDTH).astype(F32)
        squares = latents * latents
        mine[0, b:b + 1, :] = jnp.sum((squares[:, :128] + squares[:, 128:]).T, axis=0, keepdims=True)
    row_wait(0)
    row_log = -math.log2(ROWS) - log_sum(core_trade(0, log_sum(row_box[0])))

    mine[1] = row_log

    def first_column(b, carry):
        r = slice(b * CUT, (b + 1) * CUT)
        shift = spread(row_log[b:b + 1, :])
        for t in range(TILES):
            h = (score[t // 2, r, lanes_of(t)] + shift).reshape(CUT // 8, 8, 128)
            top = jnp.max(h, axis=0)
            e = jnp.exp2(h - top)
            score[t // 2, r, lanes_of(t)] = e.reshape(CUT, 128)
            gain[b, t] = top
            beta[b, t] = jnp.sum(e, axis=0)
        return carry

    for b in range(CUTS):
        first_column(b, 0)
    for t in range(TILES):
        cut_peak = gain[:, t]
        top = jnp.max(jnp.max(cut_peak, axis=0), axis=0, keepdims=True)
        sums = jnp.sum(jnp.sum(beta[:, t] * jnp.exp2(cut_peak - top), axis=0), axis=0, keepdims=True)
        col_box[me, t:t + 1, :] = top + log2(sums)
    col_trade(0)
    col_log = -math.log2(COLS) - log_sum(col_box[...])
    for t in range(TILES):
        start_gain = jnp.exp2(gain[:, t] + col_log[t:t + 1, :])
        gain[:, t] = start_gain
        beta[:, t] = start_gain

    alpha = None
    for turn in range(1, ITERS):
        for b in range(CUTS):
            r = slice(b * CUT, (b + 1) * CUT)
            acc = None
            for t in range(TILES):
                term = score[t // 2, r, lanes_of(t)].reshape(CUT // 8, 8, 128) * beta[b, t]
                acc = term if acc is None else acc + term
            row_box[turn, z, b:b + 1, :] = jnp.sum(acc.reshape(CUT, 128).T, axis=0, keepdims=True)
        row_start(turn)
        row_wait(turn)
        pair = core_trade(turn, jnp.sum(row_box[turn], axis=0))
        alpha = 1.0 / (ROWS * (pair[0] + pair[1]))

        sums = [None] * TILES
        for b in range(CUTS):
            r = slice(b * CUT, (b + 1) * CUT)
            weight = spread(alpha[b:b + 1, :])
            if turn == ITERS - 1:
                total[r, :] = weight
            for t in range(TILES):
                term = score[t // 2, r, lanes_of(t)] * weight
                term = jnp.sum(term.reshape(CUT // 8, 8, 128), axis=0) * gain[b, t]
                sums[t] = term if b == 0 else sums[t] + term
        sums = [jnp.sum(part, axis=0, keepdims=True) for part in sums]
        sum_box[turn - 1, me] = jnp.concatenate(sums, axis=0).astype(BF16)
        col_trade(turn)
        factor = 1.0 / (COLS * jnp.sum(sum_box[turn - 1].astype(F32), axis=0))
        for t in range(TILES):
            beta[:, t] = gain[:, t] * factor[t:t + 1, :]

    order = [4, 3, 5, 2, 6, 7, 1, 0]

    def project(which, group):
        for k in range(4):
            pz = zs[order[4 * group + k]]
            r = pl.ds(pl.multiple_of(pz * CUT + which * SHARE, SHARE), SHARE)
            weight = total[r, :]
            acc = None
            for t in range(TILES):
                p = (score[t // 2, r, lanes_of(t)] * weight).reshape(SHARE // 8, 8, 128) * beta[pz, t]
                acc = p if acc is None else acc + p
                plan[k * SHARE:(k + 1) * SHARE, t * 128:t * 128 + 128] = p.reshape(SHARE, 128).astype(BF16)
            peak[r, :] = acc.reshape(SHARE, 128)
        return jnp.dot(plan[...], tall[...], preferred_element_type=F32)

    for group in range(2):
        gifts[0, group] = project(other, group).astype(BF16)
        send(gifts.at[0, group], gifts.at[1, group], s_gift.at[group], r_gift.at[group], sibling)
    for group in range(2):
        numer = project(c, group)
        wait(gifts.at[1, group], r_gift.at[group])
        numer = (numer + gifts[1, group].astype(F32)).astype(BF16)
        for k in range(4):
            d = order[4 * group + k]
            boxes[0, d] = numer[k * SHARE:(k + 1) * SHARE, :]
            if d:
                send(boxes.at[0, d], boxes.at[1, z], s_box.at[0], r_box.at[0], (n, along[d]))
    boxes[1, z] = boxes[0, 0]
    for b in range(CUTS):
        row_box[ITERS, z, b:b + 1, :] = jnp.sum(peak[b * CUT:(b + 1) * CUT, :].T, axis=0, keepdims=True)
    row_start(ITERS)

    row_pot[y] = COST * mine[0] + LN2 * (row_log + log2(alpha))
    col_pot[c] = LN2 * (col_log + log2(factor))
    for d in ring:
        send(row_pot.at[y], row_pot.at[y], s_rpot.at[0], r_rpot.at[0], (n, across[d]))
    send(col_pot.at[c], col_pot.at[c], s_cpot.at[0], r_cpot.at[0], sibling)
    wait(col_pot.at[other], r_cpot.at[0])
    for pc in range(NC):
        for q in range(HALF // 128):
            col_out[4 * pc + q:4 * pc + q + 1, :] = col_pot[pc, pl.ds(4 * y + q, 1), :]
    wait(row_pot.at[0:NY - 1], r_rpot.at[0])
    low = lax.broadcasted_iota(jnp.int32, (NZ // 2, 128), 1) < SHARE
    for py in range(NY):
        pairs = row_pot[py].reshape(NZ // 2, 2, 128)
        even, odd = pairs[:, 0], pairs[:, 1]
        even_low = jnp.where(c == 0, even, pltpu.roll(even, SHARE, 1))
        odd_high = jnp.where(c == 0, pltpu.roll(odd, SHARE, 1), odd)
        row_out[4 * py:4 * py + 4, :] = jnp.where(low, even_low, odd_high)

    row_wait(ITERS)
    pair = core_trade(ITERS, jnp.sum(row_box[ITERS], axis=0))
    mine[1] = pair[0] + pair[1]
    total[0:128, :] = spread(mine[1, pl.ds(z, 1), :])
    mass = total[pl.ds(pl.multiple_of(c * SHARE, SHARE), SHARE), :]
    wait(boxes.at[1, 0:NZ - 1], r_box.at[0])
    numer = jnp.sum(boxes[1].astype(F32), axis=0)
    target_out[:, :128] = (numer[:, :128] / mass).astype(BF16)
    target_out[:, 128:] = (numer[:, 128:] / mass).astype(BF16)

    wait(offer, s_offer.at[0])
    wait(cols.at[0, 0:3], s_x.at[0])
    wait(cols.at[0, 0:3], s_y.at[0])
    wait(cols.at[0:3, 0:3, 0], s_xy.at[0])
    wait(cols.at[0:3, 0:3, 0], s_yx.at[0])
    wait(rows_x.at[0:NZ - 1, 0], s_rows.at[0])
    wait(rows_x.at[:, 0], s_pair.at[0])
    for turn in range(ITERS + 1):
        wait(row_box.at[turn, 0:NZ - 1], s_row.at[turn])
        wait(core_box.at[turn, c], s_core.at[turn])
    for turn in range(ITERS):
        wait((col_box if turn == 0 else sum_box.at[turn - 1]).at[0:GROUP - 1], s_col.at[turn])
    wait(row_pot.at[0:NY - 1], s_rpot.at[0])
    wait(col_pot.at[c], s_cpot.at[0])
    for group in range(2):
        wait(gifts.at[0, group], s_gift.at[group])
    wait(boxes.at[1, 0:NZ - 1], s_box.at[0])


def give(a, b, c, a_out, b_out, c_out, sems):
    copies = [pltpu.make_async_copy(src, dst, sems.at[k])
              for k, (src, dst) in enumerate(((a, a_out), (b, b_out), (c, c_out)))]
    for copy in copies:
        copy.start()
    for copy in copies:
        copy.wait()


def shards(noise_latents, teacher_latent_rows):
    vmem = pl.BlockSpec(memory_space=pltpu.VMEM)
    hbm = pl.BlockSpec(memory_space=pltpu.HBM)
    dma = pltpu.SemaphoreType.DMA
    shapes = (
        jax.ShapeDtypeStruct((16, 128), F32),
        jax.ShapeDtypeStruct((8, 128), F32),
        jax.ShapeDtypeStruct((SHARE, WIDTH), BF16),
    )
    results = pl.pallas_call(
        kernel,
        out_shape=shapes,
        in_specs=[hbm, hbm],
        out_specs=(vmem, vmem, vmem),
        scratch_shapes=[
            pltpu.VMEM((FEATURES, HALF), BF16),
            pltpu.VMEM((NY, NX, NC, FEATURES, HALF), BF16),
            pltpu.VMEM((NZ, NC, SHARE, WIDTH), BF16),
            pltpu.VMEM((PIECES, 1, PIECE), F32),
            pltpu.VMEM((PIECES * PIECE, WIDTH), BF16),
            pltpu.VMEM((PIECES, BLOCK_ROWS, PIECE), F32),
            pltpu.VMEM((BLOCK_ROWS, 128), F32),
            pltpu.VMEM((BLOCK_ROWS, 128), F32),
            pltpu.VMEM((CUTS, TILES, 8, 128), F32),
            pltpu.VMEM((CUTS, TILES, 8, 128), F32),
            pltpu.VMEM((4 * SHARE, PIECES * PIECE), BF16),
            pltpu.VMEM((ITERS + 1, NZ, 8, 128), F32),
            pltpu.VMEM((ITERS + 1, NC, 8, 128), F32),
            pltpu.VMEM((GROUP, TILES, 128), F32),
            pltpu.VMEM((ITERS - 1, GROUP, TILES, 128), BF16),
            pltpu.VMEM((NY, 8, 128), F32),
            pltpu.VMEM((NC, TILES, 128), F32),
            pltpu.VMEM((2, 8, 128), F32),
            pltpu.VMEM((2, 2, 4 * SHARE, WIDTH), BF16),
            pltpu.VMEM((2, NZ, SHARE, WIDTH), BF16),
            dma((3,)),
            dma((1,)), dma((1,)),
            dma((1,)), dma((1,)), dma((NX,)), dma((NY,)),
            dma((1,)), dma((1,)), dma((NY,)), dma((NY,)),
            dma((1,)), dma((NZ,)),
            dma((1,)), dma((NZ,)),
            dma((ITERS + 1,)), dma((ITERS + 1,)),
            dma((ITERS + 1,)), dma((ITERS + 1,)),
            dma((ITERS,)), dma((ITERS,)),
            dma((1,)), dma((1,)),
            dma((1,)), dma((1,)),
            dma((2,)), dma((2,)),
            dma((1,)), dma((1,)),
        ],
        compiler_params=pltpu.CompilerParams(
            collective_id=0, has_side_effects=True, vmem_limit_bytes=55172 * 1024),
        name="sinkhorn",
    )(noise_latents, teacher_latent_rows.T)
    row_pot, col_pot, targets = pl.pallas_call(
        give,
        out_shape=shapes,
        in_specs=[vmem, vmem, vmem],
        out_specs=(hbm, hbm, hbm),
        scratch_shapes=[dma((3,))],
        compiler_params=pltpu.CompilerParams(vmem_limit_bytes=2**20),
        name="give",
    )(*results)
    return row_pot.reshape(2048), col_pot.reshape(1024), targets


def solution(mesh):
    return jax.shard_map(
        shards,
        mesh=mesh,
        in_specs=(P(("noise", "sample"), None), P("sample", "noise")),
        out_specs=(P("noise"), P("sample"), P(("noise", "sample"), None)),
        check_vma=False,
    )
```

```python
import math

import jax
import jax.numpy as jnp
from jax import lax
from jax.experimental import pallas as pl
from jax.experimental.pallas import tpu as pltpu
from jax.sharding import PartitionSpec as P

ITERS = 3
WIDTH = 256
ROWS, COLS = 16384, 32768
STRENGTH = 0.1
NX, NY, NZ, NC = 4, 4, 8, 2
GROUP = NX * NY
SHARE = 64
BLOCK_ROWS = NZ * NC * SHARE
HALF = 512
FEATURES = WIDTH // (NX * NC)
PIECE = 256
PIECES = NY * HALF // PIECE
CUT = NC * SHARE
CUTS = NZ
TILES = PIECES * PIECE // 128
MESH = pl.DeviceIdType.MESH
F32, BF16 = jnp.float32, jnp.bfloat16
LN2 = math.log(2.0)
COST = 1.0 / (WIDTH * STRENGTH)


def spread(row):
    return jnp.broadcast_to(row, (128, 128)).T


def log2(a):
    return jnp.log(a) * (1.0 / LN2)


def lanes_of(t):
    return slice((t % 2) * 128, (t % 2) * 128 + 128)


def kernel(noise_hbm, teach_hbm, row_out, col_out, target_out, offer, cols, rows_x, norms, tall, score, peak, total,
           gain, beta, plan, row_box, core_box, col_box, sum_box, row_pot, col_pot, mine, gifts, boxes,
           load, s_offer, r_offer, s_x, s_y, r_x, r_y, s_xy, s_yx, r_xy, r_yx, s_rows, r_rows, s_pair, r_pair,
           s_row, r_row, s_core, r_core, s_col, r_col, s_rpot, r_rpot, s_cpot, r_cpot, s_gift, r_gift, s_box, r_box):
    n, s = lax.axis_index("noise"), lax.axis_index("sample")
    x, c = lax.div(n, NC), lax.rem(n, NC)
    y, z = lax.div(s, NZ), lax.rem(s, NZ)
    me = x * NY + y
    other = 1 - c
    xs = [x] + [lax.rem(x + d, NX) for d in range(1, NX)]
    ys = [y] + [lax.rem(y + d, NY) for d in range(1, NY)]
    zs = [z] + [lax.rem(z + d, NZ) for d in range(1, NZ)]
    noise_at = [px * NC + c for px in xs]
    across = [py * NZ + z for py in ys]
    along = [y * NZ + pz for pz in zs]
    sibling = (x * NC + other, s)
    ring = [1, 3, 2]
    near = [1, 7, 2, 6, 3, 5, 4]
    far = near[::-1]
    corner = sorted(range(1, GROUP), key=lambda k: -(min(k // NY, NX - k // NY) + min(k % NY, NY - k % NY)))
    xy = [(noise_at[k // NY], across[k % NY]) for k in corner]

    def send(src, dst, send_sem, recv_sem, device):
        pltpu.make_async_remote_copy(src_ref=src, dst_ref=dst, send_sem=send_sem, recv_sem=recv_sem,
                                     device_id=device, device_id_type=MESH).start()

    def wait(ref, sem):
        pltpu.make_async_copy(ref, ref, sem).wait()

    def half(which):
        return teach_hbm.at[:, pl.ds(pl.multiple_of(which * HALF, HALF), HALF)]

    own = cols.at[y, x, c]
    theirs = cols.at[y, x, other]
    loads = [pltpu.make_async_copy(half(other), offer, load.at[0]),
             pltpu.make_async_copy(half(c), own, load.at[1]),
             pltpu.make_async_copy(noise_hbm, rows_x.at[z, c], load.at[2])]
    for copy in loads:
        copy.start()

    barrier = pltpu.get_barrier_semaphore()
    greeted = xy[:1] + [(n, along[d]) for d in far] + xy[1:] + [sibling]
    for device in greeted:
        pl.semaphore_signal(barrier, inc=1, device_id=device, device_id_type=MESH)
    peak[...] = jnp.full((BLOCK_ROWS, 128), -1e30, F32)
    total[...] = jnp.zeros((BLOCK_ROWS, 128), F32)
    for copy in loads:
        copy.wait()
    pl.semaphore_wait(barrier, len(greeted))

    send(offer, cols.at[y, x, c], s_offer.at[0], r_offer.at[0], sibling)
    for d in ring:
        send(own, own, s_x.at[0], r_x.at[x], (noise_at[d], s))
        send(own, own, s_x.at[0], r_xy.at[y], (n, across[d]))
    for d in near:
        send(rows_x.at[z, c], rows_x.at[z, c], s_rows.at[0], r_rows.at[z], (n, along[d]))
    send(rows_x.at[z, c], rows_x.at[z, c], s_pair.at[0], r_pair.at[z], sibling)
    wait(theirs, r_offer.at[0])
    for d in ring:
        send(theirs, theirs, s_y.at[0], r_y.at[y], (n, across[d]))
        send(theirs, theirs, s_y.at[0], r_yx.at[y], (noise_at[d], s))
    for d in ring:
        wait(cols.at[y, xs[d], c], r_x.at[xs[d]])
    for q in (3, 1, 2):
        for d in ring:
            passed = cols.at[y, xs[d], c]
            send(passed, passed, s_xy.at[0], r_xy.at[y], (n, across[NY - q]))
        passed = cols.at[ys[q], x, other]
        wait(passed, r_y.at[ys[q]])
        for e in ring:
            send(passed, passed, s_yx.at[0], r_yx.at[ys[q]], (noise_at[e], s))
    def block_of(py, part):
        return cols[py, :, :, :, part * PIECE:(part + 1) * PIECE].reshape(WIDTH, PIECE)

    def norms_of(py):
        for part in range(2):
            wide = block_of(py, part).astype(F32)
            norms[py * 2 + part] = jnp.sum(wide * wide, axis=0, keepdims=True) * (COST / LN2)

    def scores_of(py, blocks):
        for b in blocks:
            r = slice(b * CUT, (b + 1) * CUT) if isinstance(b, int) else pl.ds(pl.multiple_of(b * CUT, CUT), CUT)
            latents = rows_x[b].reshape(CUT, WIDTH)
            tiles = []
            for part in range(2):
                dots = jnp.dot(latents, block_of(py, part), preferred_element_type=F32)
                h = dots * (2.0 * COST / LN2) - norms[py * 2 + part]
                score[py * 2 + part, r, :] = h
                tiles += [h[:, :128], h[:, 128:]]
            old = peak[r, :]
            new = jnp.maximum(jnp.maximum(tiles[0], tiles[1]), jnp.maximum(tiles[2], tiles[3]))
            new = jnp.maximum(old, new)
            sums = [jnp.exp2(tile - new) for tile in tiles]
            total[r, :] = total[r, :] * jnp.exp2(old - new) + ((sums[0] + sums[1]) + (sums[2] + sums[3]))
            peak[r, :] = new

    def piece_wait(py):
        wait(cols.at[py, :, c], r_xy.at[py])
        wait(cols.at[py, 0:NX - 1, other], r_yx.at[py])
        norms_of(py)

    def off(k):
        return lax.rem(z + lax.div(k + 1, 2) * (2 * lax.rem(k, 2) - 1) + NZ, NZ)

    wait(cols.at[y, 0:NX - 1, other], r_yx.at[y])
    norms_of(y)

    def rows_in(k, carry):
        pz, last = off(k), off(k - 1)
        passed = rows_x.at[pz, c]
        wait(passed, r_rows.at[pz])
        send(passed, passed, s_pair.at[0], r_pair.at[pz], sibling)
        wait(rows_x.at[last, other], r_pair.at[last])
        scores_of(y, [last])
        return carry

    lax.fori_loop(1, NZ, rows_in, 0)
    wait(rows_x.at[zs[4], other], r_pair.at[zs[4]])
    scores_of(y, [zs[4]])

    def piece(k, carry):
        py = lax.rem(y + lax.div(3 * k * (k + 1), 2), NY)
        piece_wait(py)
        scores_of(py, range(CUTS))
        return carry

    lax.fori_loop(1, NY, piece, 0)

    def row_start(turn):
        for d in far:
            send(row_box.at[turn, z], row_box.at[turn, z], s_row.at[turn], r_row.at[turn], (n, along[d]))

    def row_wait(turn):
        wait(row_box.at[turn, 0:NZ - 1], r_row.at[turn])

    def core_trade(turn, value):
        core_box[turn, c] = value
        send(core_box.at[turn, c], core_box.at[turn, c], s_core.at[turn], r_core.at[turn], sibling)
        wait(core_box.at[turn, other], r_core.at[turn])
        return core_box[turn]

    def col_trade(turn):
        box = col_box if turn == 0 else sum_box.at[turn - 1]
        for device in xy:
            send(box.at[me], box.at[me], s_col.at[turn], r_col.at[turn], device)
        wait(box.at[0:GROUP - 1], r_col.at[turn])

    def log_sum(logs):
        top = jnp.max(logs, axis=0)
        return top + log2(jnp.sum(jnp.exp2(logs - top), axis=0))

    for b in range(CUTS):
        r = slice(b * CUT, (b + 1) * CUT)
        lane_peak = peak[r, :].T
        lane_total = total[r, :].T
        top = jnp.max(lane_peak, axis=0, keepdims=True)
        sums = jnp.sum(lane_total * jnp.exp2(lane_peak - top), axis=0, keepdims=True)
        row_box[0, z, b:b + 1, :] = top + log2(sums)
    row_start(0)
    for u in range(PIECES):
        tall[u * PIECE:(u + 1) * PIECE, :] = block_of(u // 2, u % 2).astype(F32).T.astype(BF16)
    for b in range(CUTS):
        latents = rows_x[b].reshape(CUT, WIDTH).astype(F32)
        squares = latents * latents
        mine[0, b:b + 1, :] = jnp.sum((squares[:, :128] + squares[:, 128:]).T, axis=0, keepdims=True)
    row_wait(0)
    row_log = -math.log2(ROWS) - log_sum(core_trade(0, log_sum(row_box[0])))

    mine[1] = row_log

    def first_column(b, carry):
        r = slice(b * CUT, (b + 1) * CUT)
        shift = spread(row_log[b:b + 1, :])
        for t in range(TILES):
            h = (score[t // 2, r, lanes_of(t)] + shift).reshape(CUT // 8, 8, 128)
            top = jnp.max(h, axis=0)
            e = jnp.exp2(h - top)
            score[t // 2, r, lanes_of(t)] = e.reshape(CUT, 128)
            gain[b, t] = top
            beta[b, t] = jnp.sum(e, axis=0)
        return carry

    for b in range(CUTS):
        first_column(b, 0)
    for t in range(TILES):
        cut_peak = gain[:, t]
        top = jnp.max(jnp.max(cut_peak, axis=0), axis=0, keepdims=True)
        sums = jnp.sum(jnp.sum(beta[:, t] * jnp.exp2(cut_peak - top), axis=0), axis=0, keepdims=True)
        col_box[me, t:t + 1, :] = top + log2(sums)
    col_trade(0)
    col_log = -math.log2(COLS) - log_sum(col_box[...])
    for t in range(TILES):
        start_gain = jnp.exp2(gain[:, t] + col_log[t:t + 1, :])
        gain[:, t] = start_gain
        beta[:, t] = start_gain

    def row_sums_into(turn, scale):
        for b in range(CUTS):
            r = slice(b * CUT, (b + 1) * CUT)
            acc = None
            for t in range(TILES):
                term = score[t // 2, r, lanes_of(t)].reshape(CUT // 8, 8, 128) * beta[b, t]
                acc = term if acc is None else acc + term
            sums = jnp.sum(acc.reshape(CUT, 128).T, axis=0, keepdims=True)
            row_box[turn, z, b:b + 1, :] = sums if scale is None else sums * scale[b:b + 1, :]

    alpha = None
    for turn in range(1, ITERS):
        row_sums_into(turn, None)
        row_start(turn)
        row_wait(turn)
        pair = core_trade(turn, jnp.sum(row_box[turn], axis=0))
        alpha = 1.0 / (ROWS * (pair[0] + pair[1]))

        sums = [None] * TILES
        for b in range(CUTS):
            r = slice(b * CUT, (b + 1) * CUT)
            weight = spread(alpha[b:b + 1, :])
            if turn == ITERS - 1:
                total[r, :] = weight
            for t in range(TILES):
                term = score[t // 2, r, lanes_of(t)] * weight
                term = jnp.sum(term.reshape(CUT // 8, 8, 128), axis=0) * gain[b, t]
                sums[t] = term if b == 0 else sums[t] + term
        sums = [jnp.sum(part, axis=0, keepdims=True) for part in sums]
        sum_box[turn - 1, me] = jnp.concatenate(sums, axis=0).astype(BF16)
        col_trade(turn)
        factor = 1.0 / (COLS * jnp.sum(sum_box[turn - 1].astype(F32), axis=0))
        for t in range(TILES):
            beta[:, t] = gain[:, t] * factor[t:t + 1, :]

    order = [4, 3, 5, 2, 6, 7, 1, 0]

    def project(which, group):
        for k in range(4):
            pz = zs[order[4 * group + k]]
            r = pl.ds(pl.multiple_of(pz * CUT + which * SHARE, SHARE), SHARE)
            weight = total[r, :]
            for t in range(TILES):
                p = (score[t // 2, r, lanes_of(t)] * weight).reshape(SHARE // 8, 8, 128) * beta[pz, t]
                plan[k * SHARE:(k + 1) * SHARE, t * 128:t * 128 + 128] = p.reshape(SHARE, 128).astype(BF16)
        return jnp.dot(plan[...], tall[...], preferred_element_type=F32)

    row_sums_into(ITERS, alpha)
    row_start(ITERS)
    for group in range(2):
        gifts[0, group] = project(other, group).astype(BF16)
        send(gifts.at[0, group], gifts.at[1, group], s_gift.at[group], r_gift.at[group], sibling)
    for group in range(2):
        numer = project(c, group)
        wait(gifts.at[1, group], r_gift.at[group])
        numer = (numer + gifts[1, group].astype(F32)).astype(BF16)
        for k in range(4):
            d = order[4 * group + k]
            boxes[0, d] = numer[k * SHARE:(k + 1) * SHARE, :]
            if d:
                send(boxes.at[0, d], boxes.at[1, z], s_box.at[0], r_box.at[0], (n, along[d]))
    boxes[1, z] = boxes[0, 0]

    row_pot[y] = COST * mine[0] + LN2 * (row_log + log2(alpha))
    col_pot[c] = LN2 * (col_log + log2(factor))
    for d in ring:
        send(row_pot.at[y], row_pot.at[y], s_rpot.at[0], r_rpot.at[0], (n, across[d]))
    send(col_pot.at[c], col_pot.at[c], s_cpot.at[0], r_cpot.at[0], sibling)
    wait(col_pot.at[other], r_cpot.at[0])
    for pc in range(NC):
        for q in range(HALF // 128):
            col_out[4 * pc + q:4 * pc + q + 1, :] = col_pot[pc, pl.ds(4 * y + q, 1), :]
    wait(row_pot.at[0:NY - 1], r_rpot.at[0])
    low = lax.broadcasted_iota(jnp.int32, (NZ // 2, 128), 1) < SHARE
    for py in range(NY):
        pairs = row_pot[py].reshape(NZ // 2, 2, 128)
        even, odd = pairs[:, 0], pairs[:, 1]
        even_low = jnp.where(c == 0, even, pltpu.roll(even, SHARE, 1))
        odd_high = jnp.where(c == 0, pltpu.roll(odd, SHARE, 1), odd)
        row_out[4 * py:4 * py + 4, :] = jnp.where(low, even_low, odd_high)

    row_wait(ITERS)
    pair = core_trade(ITERS, jnp.sum(row_box[ITERS], axis=0))
    mine[1] = pair[0] + pair[1]
    total[0:128, :] = spread(mine[1, pl.ds(z, 1), :])
    mass = total[pl.ds(pl.multiple_of(c * SHARE, SHARE), SHARE), :]
    wait(boxes.at[1, 0:NZ - 1], r_box.at[0])
    numer = jnp.sum(boxes[1].astype(F32), axis=0)
    target_out[:, :128] = (numer[:, :128] / mass).astype(BF16)
    target_out[:, 128:] = (numer[:, 128:] / mass).astype(BF16)

    wait(offer, s_offer.at[0])
    wait(cols.at[0, 0:3], s_x.at[0])
    wait(cols.at[0, 0:3], s_y.at[0])
    wait(cols.at[0:3, 0:3, 0], s_xy.at[0])
    wait(cols.at[0:3, 0:3, 0], s_yx.at[0])
    wait(rows_x.at[0:NZ - 1, 0], s_rows.at[0])
    wait(rows_x.at[:, 0], s_pair.at[0])
    for turn in range(ITERS + 1):
        wait(row_box.at[turn, 0:NZ - 1], s_row.at[turn])
        wait(core_box.at[turn, c], s_core.at[turn])
    for turn in range(ITERS):
        wait((col_box if turn == 0 else sum_box.at[turn - 1]).at[0:GROUP - 1], s_col.at[turn])
    wait(row_pot.at[0:NY - 1], s_rpot.at[0])
    wait(col_pot.at[c], s_cpot.at[0])
    for group in range(2):
        wait(gifts.at[0, group], s_gift.at[group])
    wait(boxes.at[1, 0:NZ - 1], s_box.at[0])


def give(a, b, c, a_out, b_out, c_out, sems):
    copies = [pltpu.make_async_copy(src, dst, sems.at[k])
              for k, (src, dst) in enumerate(((a, a_out), (b, b_out), (c, c_out)))]
    for copy in copies:
        copy.start()
    for copy in copies:
        copy.wait()


def shards(noise_latents, teacher_latent_rows):
    vmem = pl.BlockSpec(memory_space=pltpu.VMEM)
    hbm = pl.BlockSpec(memory_space=pltpu.HBM)
    dma = pltpu.SemaphoreType.DMA
    shapes = (
        jax.ShapeDtypeStruct((16, 128), F32),
        jax.ShapeDtypeStruct((8, 128), F32),
        jax.ShapeDtypeStruct((SHARE, WIDTH), BF16),
    )
    results = pl.pallas_call(
        kernel,
        out_shape=shapes,
        in_specs=[hbm, hbm],
        out_specs=(vmem, vmem, vmem),
        scratch_shapes=[
            pltpu.VMEM((FEATURES, HALF), BF16),
            pltpu.VMEM((NY, NX, NC, FEATURES, HALF), BF16),
            pltpu.VMEM((NZ, NC, SHARE, WIDTH), BF16),
            pltpu.VMEM((PIECES, 1, PIECE), F32),
            pltpu.VMEM((PIECES * PIECE, WIDTH), BF16),
            pltpu.VMEM((PIECES, BLOCK_ROWS, PIECE), F32),
            pltpu.VMEM((BLOCK_ROWS, 128), F32),
            pltpu.VMEM((BLOCK_ROWS, 128), F32),
            pltpu.VMEM((CUTS, TILES, 8, 128), F32),
            pltpu.VMEM((CUTS, TILES, 8, 128), F32),
            pltpu.VMEM((4 * SHARE, PIECES * PIECE), BF16),
            pltpu.VMEM((ITERS + 1, NZ, 8, 128), F32),
            pltpu.VMEM((ITERS + 1, NC, 8, 128), F32),
            pltpu.VMEM((GROUP, TILES, 128), F32),
            pltpu.VMEM((ITERS - 1, GROUP, TILES, 128), BF16),
            pltpu.VMEM((NY, 8, 128), F32),
            pltpu.VMEM((NC, TILES, 128), F32),
            pltpu.VMEM((2, 8, 128), F32),
            pltpu.VMEM((2, 2, 4 * SHARE, WIDTH), BF16),
            pltpu.VMEM((2, NZ, SHARE, WIDTH), BF16),
            dma((3,)),
            dma((1,)), dma((1,)),
            dma((1,)), dma((1,)), dma((NX,)), dma((NY,)),
            dma((1,)), dma((1,)), dma((NY,)), dma((NY,)),
            dma((1,)), dma((NZ,)),
            dma((1,)), dma((NZ,)),
            dma((ITERS + 1,)), dma((ITERS + 1,)),
            dma((ITERS + 1,)), dma((ITERS + 1,)),
            dma((ITERS,)), dma((ITERS,)),
            dma((1,)), dma((1,)),
            dma((1,)), dma((1,)),
            dma((2,)), dma((2,)),
            dma((1,)), dma((1,)),
        ],
        compiler_params=pltpu.CompilerParams(
            collective_id=0, has_side_effects=True, vmem_limit_bytes=55172 * 1024),
        name="sinkhorn",
    )(noise_latents, teacher_latent_rows.T)
    row_pot, col_pot, targets = pl.pallas_call(
        give,
        out_shape=shapes,
        in_specs=[vmem, vmem, vmem],
        out_specs=(hbm, hbm, hbm),
        scratch_shapes=[dma((3,))],
        compiler_params=pltpu.CompilerParams(vmem_limit_bytes=2**20),
        name="give",
    )(*results)
    return row_pot.reshape(2048), col_pot.reshape(1024), targets


def solution(mesh):
    return jax.shard_map(
        shards,
        mesh=mesh,
        in_specs=(P(("noise", "sample"), None), P("sample", "noise")),
        out_specs=(P("noise"), P("sample"), P(("noise", "sample"), None)),
        check_vma=False,
    )
```

```python
import math

import jax
import jax.numpy as jnp
from jax import lax
from jax.experimental import pallas as pl
from jax.experimental.pallas import tpu as pltpu
from jax.sharding import PartitionSpec as P

ITERS = 3
WIDTH = 256
ROWS, COLS = 16384, 32768
STRENGTH = 0.1
NX, NY, NZ, NC = 4, 4, 8, 2
GROUP = NX * NY
SHARE = 64
BLOCK_ROWS = NZ * NC * SHARE
HALF = 512
FEATURES = WIDTH // (NX * NC)
PIECE = 256
PIECES = NY * HALF // PIECE
CUT = NC * SHARE
CUTS = NZ
TILES = PIECES * PIECE // 128
MESH = pl.DeviceIdType.MESH
F32, BF16 = jnp.float32, jnp.bfloat16
LN2 = math.log(2.0)
COST = 1.0 / (WIDTH * STRENGTH)


def spread(row):
    return jnp.broadcast_to(row, (128, 128)).T


def log2(a):
    return jnp.log(a) * (1.0 / LN2)


def lanes_of(t):
    return slice((t % 2) * 128, (t % 2) * 128 + 128)


def kernel(noise_hbm, teach_hbm, row_out, col_out, target_out, offer, cols, rows_x, norms, tall, score, peak, total,
           gain, beta, plan, row_box, core_box, col_box, sum_box, row_pot, col_pot, mine, gifts, boxes,
           load, s_offer, r_offer, s_x, s_y, r_x, r_y, s_xy, s_yx, r_xy, r_yx, s_rows, r_rows, s_pair, r_pair,
           s_row, r_row, s_core, r_core, s_col, r_col, s_rpot, r_rpot, s_cpot, r_cpot, s_gift, r_gift, s_box, r_box):
    n, s = lax.axis_index("noise"), lax.axis_index("sample")
    x, c = lax.div(n, NC), lax.rem(n, NC)
    y, z = lax.div(s, NZ), lax.rem(s, NZ)
    me = x * NY + y
    other = 1 - c
    xs = [x] + [lax.rem(x + d, NX) for d in range(1, NX)]
    ys = [y] + [lax.rem(y + d, NY) for d in range(1, NY)]
    zs = [z] + [lax.rem(z + d, NZ) for d in range(1, NZ)]
    noise_at = [px * NC + c for px in xs]
    across = [py * NZ + z for py in ys]
    along = [y * NZ + pz for pz in zs]
    sibling = (x * NC + other, s)
    ring = [1, 3, 2]
    near = [1, 7, 2, 6, 3, 5, 4]
    far = near[::-1]
    corner = sorted(range(1, GROUP), key=lambda k: -(min(k // NY, NX - k // NY) + min(k % NY, NY - k % NY)))
    xy = [(noise_at[k // NY], across[k % NY]) for k in corner]

    def send(src, dst, send_sem, recv_sem, device):
        pltpu.make_async_remote_copy(src_ref=src, dst_ref=dst, send_sem=send_sem, recv_sem=recv_sem,
                                     device_id=device, device_id_type=MESH).start()

    def wait(ref, sem):
        pltpu.make_async_copy(ref, ref, sem).wait()

    def half(which):
        return teach_hbm.at[:, pl.ds(pl.multiple_of(which * HALF, HALF), HALF)]

    own = cols.at[y, x, c]
    theirs = cols.at[y, x, other]
    loads = [pltpu.make_async_copy(half(other), offer, load.at[0]),
             pltpu.make_async_copy(half(c), own, load.at[1]),
             pltpu.make_async_copy(noise_hbm, rows_x.at[z, c], load.at[2])]
    for copy in loads:
        copy.start()

    barrier = pltpu.get_barrier_semaphore()
    greeted = xy[:1] + [(n, along[d]) for d in far] + xy[1:] + [sibling]
    for device in greeted:
        pl.semaphore_signal(barrier, inc=1, device_id=device, device_id_type=MESH)
    peak[...] = jnp.full((BLOCK_ROWS, 128), -1e30, F32)
    total[...] = jnp.zeros((BLOCK_ROWS, 128), F32)
    for copy in loads:
        copy.wait()
    pl.semaphore_wait(barrier, len(greeted))

    send(offer, cols.at[y, x, c], s_offer.at[0], r_offer.at[0], sibling)
    for d in ring:
        send(own, own, s_x.at[0], r_x.at[x], (noise_at[d], s))
        send(own, own, s_x.at[0], r_xy.at[y], (n, across[d]))
    for d in near:
        send(rows_x.at[z, c], rows_x.at[z, c], s_rows.at[0], r_rows.at[z], (n, along[d]))
    send(rows_x.at[z, c], rows_x.at[z, c], s_pair.at[0], r_pair.at[z], sibling)
    wait(theirs, r_offer.at[0])
    for d in ring:
        send(theirs, theirs, s_y.at[0], r_y.at[y], (n, across[d]))
        send(theirs, theirs, s_y.at[0], r_yx.at[y], (noise_at[d], s))
    for d in ring:
        wait(cols.at[y, xs[d], c], r_x.at[xs[d]])
    for q in (3, 1, 2):
        for d in ring:
            passed = cols.at[y, xs[d], c]
            send(passed, passed, s_xy.at[0], r_xy.at[y], (n, across[NY - q]))
        passed = cols.at[ys[q], x, other]
        wait(passed, r_y.at[ys[q]])
        for e in ring:
            send(passed, passed, s_yx.at[0], r_yx.at[ys[q]], (noise_at[e], s))
    def block_of(py, part):
        return cols[py, :, :, :, part * PIECE:(part + 1) * PIECE].reshape(WIDTH, PIECE)

    def norms_of(py):
        for part in range(2):
            wide = block_of(py, part).astype(F32)
            norms[py * 2 + part] = jnp.sum(wide * wide, axis=0, keepdims=True) * (COST / LN2)

    def scores_of(py, blocks):
        for b in blocks:
            r = slice(b * CUT, (b + 1) * CUT) if isinstance(b, int) else pl.ds(pl.multiple_of(b * CUT, CUT), CUT)
            latents = rows_x[b].reshape(CUT, WIDTH)
            tiles = []
            for part in range(2):
                dots = jnp.dot(latents, block_of(py, part), preferred_element_type=F32)
                h = dots * (2.0 * COST / LN2) - norms[py * 2 + part]
                score[py * 2 + part, r, :] = h
                tiles += [h[:, :128], h[:, 128:]]
            old = peak[r, :]
            new = jnp.maximum(jnp.maximum(tiles[0], tiles[1]), jnp.maximum(tiles[2], tiles[3]))
            new = jnp.maximum(old, new)
            sums = [jnp.exp2(tile - new) for tile in tiles]
            total[r, :] = total[r, :] * jnp.exp2(old - new) + ((sums[0] + sums[1]) + (sums[2] + sums[3]))
            peak[r, :] = new

    def piece_wait(py):
        wait(cols.at[py, :, c], r_xy.at[py])
        wait(cols.at[py, 0:NX - 1, other], r_yx.at[py])
        norms_of(py)

    def off(k):
        return lax.rem(z + lax.div(k + 1, 2) * (2 * lax.rem(k, 2) - 1) + NZ, NZ)

    wait(cols.at[y, 0:NX - 1, other], r_yx.at[y])
    norms_of(y)

    def rows_in(k, carry):
        pz, last = off(k), off(k - 1)
        passed = rows_x.at[pz, c]
        wait(passed, r_rows.at[pz])
        send(passed, passed, s_pair.at[0], r_pair.at[pz], sibling)
        wait(rows_x.at[last, other], r_pair.at[last])
        scores_of(y, [last])
        return carry

    lax.fori_loop(1, NZ, rows_in, 0)
    wait(rows_x.at[zs[4], other], r_pair.at[zs[4]])
    scores_of(y, [zs[4]])

    def piece(k, carry):
        py = lax.rem(y + lax.div(3 * k * (k + 1), 2), NY)
        piece_wait(py)
        scores_of(py, range(CUTS))
        return carry

    lax.fori_loop(1, NY, piece, 0)

    def row_start(turn):
        for d in far:
            send(row_box.at[turn, z], row_box.at[turn, z], s_row.at[turn], r_row.at[turn], (n, along[d]))

    def row_wait(turn):
        wait(row_box.at[turn, 0:NZ - 1], r_row.at[turn])

    def core_trade(turn, value):
        core_box[turn, c] = value
        send(core_box.at[turn, c], core_box.at[turn, c], s_core.at[turn], r_core.at[turn], sibling)
        wait(core_box.at[turn, other], r_core.at[turn])
        return core_box[turn]

    def col_trade(turn):
        box = col_box if turn == 0 else sum_box.at[turn - 1]
        for device in xy:
            send(box.at[me], box.at[me], s_col.at[turn], r_col.at[turn], device)
        wait(box.at[0:GROUP - 1], r_col.at[turn])

    def log_sum(logs):
        top = jnp.max(logs, axis=0)
        return top + log2(jnp.sum(jnp.exp2(logs - top), axis=0))

    for b in range(CUTS):
        r = slice(b * CUT, (b + 1) * CUT)
        lane_peak = peak[r, :].T
        lane_total = total[r, :].T
        top = jnp.max(lane_peak, axis=0, keepdims=True)
        sums = jnp.sum(lane_total * jnp.exp2(lane_peak - top), axis=0, keepdims=True)
        row_box[0, z, b:b + 1, :] = top + log2(sums)
    row_start(0)
    for u in range(PIECES):
        tall[u * PIECE:(u + 1) * PIECE, :] = block_of(u // 2, u % 2).astype(F32).T.astype(BF16)
    for b in range(CUTS):
        latents = rows_x[b].reshape(CUT, WIDTH).astype(F32)
        squares = latents * latents
        mine[0, b:b + 1, :] = jnp.sum((squares[:, :128] + squares[:, 128:]).T, axis=0, keepdims=True)
    row_wait(0)
    row_log = -math.log2(ROWS) - log_sum(core_trade(0, log_sum(row_box[0])))

    mine[1] = row_log

    def first_column(b, carry):
        r = slice(b * CUT, (b + 1) * CUT)
        shift = spread(row_log[b:b + 1, :])
        for t in range(TILES):
            h = (score[t // 2, r, lanes_of(t)] + shift).reshape(CUT // 8, 8, 128)
            top = jnp.max(h, axis=0)
            e = jnp.exp2(h - top)
            score[t // 2, r, lanes_of(t)] = e.reshape(CUT, 128)
            gain[b, t] = top
            beta[b, t] = jnp.sum(e, axis=0)
        return carry

    for b in range(CUTS):
        first_column(b, 0)
    for t in range(TILES):
        cut_peak = gain[:, t]
        top = jnp.max(jnp.max(cut_peak, axis=0), axis=0, keepdims=True)
        sums = jnp.sum(jnp.sum(beta[:, t] * jnp.exp2(cut_peak - top), axis=0), axis=0, keepdims=True)
        col_box[me, t:t + 1, :] = top + log2(sums)
    col_trade(0)
    col_log = -math.log2(COLS) - log_sum(col_box[...])
    for t in range(TILES):
        start_gain = jnp.exp2(gain[:, t] + col_log[t:t + 1, :])
        gain[:, t] = start_gain
        beta[:, t] = start_gain

    def row_sums_into(turn, scale):
        for b in range(CUTS):
            r = slice(b * CUT, (b + 1) * CUT)
            acc = None
            for t in range(TILES):
                term = score[t // 2, r, lanes_of(t)].reshape(CUT // 8, 8, 128) * beta[b, t]
                acc = term if acc is None else acc + term
            sums = jnp.sum(acc.reshape(CUT, 128).T, axis=0, keepdims=True)
            row_box[turn, z, b:b + 1, :] = sums if scale is None else sums * scale[b:b + 1, :]

    alpha = None
    for turn in range(1, ITERS):
        row_sums_into(turn, None)
        row_start(turn)
        row_wait(turn)
        pair = core_trade(turn, jnp.sum(row_box[turn], axis=0))
        alpha = 1.0 / (ROWS * (pair[0] + pair[1]))

        sums = [None] * TILES
        for b in range(CUTS):
            r = slice(b * CUT, (b + 1) * CUT)
            weight = spread(alpha[b:b + 1, :])
            if turn == ITERS - 1:
                total[r, :] = weight
            for t in range(TILES):
                term = score[t // 2, r, lanes_of(t)] * weight
                term = jnp.sum(term.reshape(CUT // 8, 8, 128), axis=0) * gain[b, t]
                sums[t] = term if b == 0 else sums[t] + term
        sums = [jnp.sum(part, axis=0, keepdims=True) for part in sums]
        sum_box[turn - 1, me] = jnp.concatenate(sums, axis=0).astype(BF16)
        col_trade(turn)
        factor = 1.0 / (COLS * jnp.sum(sum_box[turn - 1].astype(F32), axis=0))
        for t in range(TILES):
            beta[:, t] = gain[:, t] * factor[t:t + 1, :]

    order = [4, 3, 5, 2, 6, 7, 1, 0]

    def project(which, group):
        for k in range(4):
            pz = zs[order[4 * group + k]]
            r = pl.ds(pl.multiple_of(pz * CUT + which * SHARE, SHARE), SHARE)
            weight = total[r, :]
            for t in range(TILES):
                p = (score[t // 2, r, lanes_of(t)] * weight).reshape(SHARE // 8, 8, 128) * beta[pz, t]
                plan[k * SHARE:(k + 1) * SHARE, t * 128:t * 128 + 128] = p.reshape(SHARE, 128).astype(BF16)
        return jnp.dot(plan[...], tall[...], preferred_element_type=F32)

    def give_to_sibling(group):
        gifts[0, group] = project(other, group).astype(BF16)
        send(gifts.at[0, group], gifts.at[1, group], s_gift.at[group], r_gift.at[group], sibling)

    def give_along(group, numer):
        wait(gifts.at[1, group], r_gift.at[group])
        numer = (numer + gifts[1, group].astype(F32)).astype(BF16)
        for k in range(4):
            d = order[4 * group + k]
            boxes[0, d] = numer[k * SHARE:(k + 1) * SHARE, :]
            if d:
                send(boxes.at[0, d], boxes.at[1, z], s_box.at[0], r_box.at[0], (n, along[d]))

    give_to_sibling(0)
    row_sums_into(ITERS, alpha)
    row_start(ITERS)
    first = project(c, 0)
    give_along(0, first)
    give_to_sibling(1)
    give_along(1, project(c, 1))
    boxes[1, z] = boxes[0, 0]

    row_pot[y] = COST * mine[0] + LN2 * (row_log + log2(alpha))
    col_pot[c] = LN2 * (col_log + log2(factor))
    for d in ring:
        send(row_pot.at[y], row_pot.at[y], s_rpot.at[0], r_rpot.at[0], (n, across[d]))
    send(col_pot.at[c], col_pot.at[c], s_cpot.at[0], r_cpot.at[0], sibling)
    wait(col_pot.at[other], r_cpot.at[0])
    for pc in range(NC):
        for q in range(HALF // 128):
            col_out[4 * pc + q:4 * pc + q + 1, :] = col_pot[pc, pl.ds(4 * y + q, 1), :]
    wait(row_pot.at[0:NY - 1], r_rpot.at[0])
    low = lax.broadcasted_iota(jnp.int32, (NZ // 2, 128), 1) < SHARE
    for py in range(NY):
        pairs = row_pot[py].reshape(NZ // 2, 2, 128)
        even, odd = pairs[:, 0], pairs[:, 1]
        even_low = jnp.where(c == 0, even, pltpu.roll(even, SHARE, 1))
        odd_high = jnp.where(c == 0, pltpu.roll(odd, SHARE, 1), odd)
        row_out[4 * py:4 * py + 4, :] = jnp.where(low, even_low, odd_high)

    row_wait(ITERS)
    pair = core_trade(ITERS, jnp.sum(row_box[ITERS], axis=0))
    mine[1] = pair[0] + pair[1]
    total[0:128, :] = spread(mine[1, pl.ds(z, 1), :])
    mass = total[pl.ds(pl.multiple_of(c * SHARE, SHARE), SHARE), :]
    wait(boxes.at[1, 0:NZ - 1], r_box.at[0])
    numer = jnp.sum(boxes[1].astype(F32), axis=0)
    target_out[:, :128] = (numer[:, :128] / mass).astype(BF16)
    target_out[:, 128:] = (numer[:, 128:] / mass).astype(BF16)

    wait(offer, s_offer.at[0])
    wait(cols.at[0, 0:3], s_x.at[0])
    wait(cols.at[0, 0:3], s_y.at[0])
    wait(cols.at[0:3, 0:3, 0], s_xy.at[0])
    wait(cols.at[0:3, 0:3, 0], s_yx.at[0])
    wait(rows_x.at[0:NZ - 1, 0], s_rows.at[0])
    wait(rows_x.at[:, 0], s_pair.at[0])
    for turn in range(ITERS + 1):
        wait(row_box.at[turn, 0:NZ - 1], s_row.at[turn])
        wait(core_box.at[turn, c], s_core.at[turn])
    for turn in range(ITERS):
        wait((col_box if turn == 0 else sum_box.at[turn - 1]).at[0:GROUP - 1], s_col.at[turn])
    wait(row_pot.at[0:NY - 1], s_rpot.at[0])
    wait(col_pot.at[c], s_cpot.at[0])
    for group in range(2):
        wait(gifts.at[0, group], s_gift.at[group])
    wait(boxes.at[1, 0:NZ - 1], s_box.at[0])


def give(a, b, c, a_out, b_out, c_out, sems):
    copies = [pltpu.make_async_copy(src, dst, sems.at[k])
              for k, (src, dst) in enumerate(((a, a_out), (b, b_out), (c, c_out)))]
    for copy in copies:
        copy.start()
    for copy in copies:
        copy.wait()


def shards(noise_latents, teacher_latent_rows):
    vmem = pl.BlockSpec(memory_space=pltpu.VMEM)
    hbm = pl.BlockSpec(memory_space=pltpu.HBM)
    dma = pltpu.SemaphoreType.DMA
    shapes = (
        jax.ShapeDtypeStruct((16, 128), F32),
        jax.ShapeDtypeStruct((8, 128), F32),
        jax.ShapeDtypeStruct((SHARE, WIDTH), BF16),
    )
    results = pl.pallas_call(
        kernel,
        out_shape=shapes,
        in_specs=[hbm, hbm],
        out_specs=(vmem, vmem, vmem),
        scratch_shapes=[
            pltpu.VMEM((FEATURES, HALF), BF16),
            pltpu.VMEM((NY, NX, NC, FEATURES, HALF), BF16),
            pltpu.VMEM((NZ, NC, SHARE, WIDTH), BF16),
            pltpu.VMEM((PIECES, 1, PIECE), F32),
            pltpu.VMEM((PIECES * PIECE, WIDTH), BF16),
            pltpu.VMEM((PIECES, BLOCK_ROWS, PIECE), F32),
            pltpu.VMEM((BLOCK_ROWS, 128), F32),
            pltpu.VMEM((BLOCK_ROWS, 128), F32),
            pltpu.VMEM((CUTS, TILES, 8, 128), F32),
            pltpu.VMEM((CUTS, TILES, 8, 128), F32),
            pltpu.VMEM((4 * SHARE, PIECES * PIECE), BF16),
            pltpu.VMEM((ITERS + 1, NZ, 8, 128), F32),
            pltpu.VMEM((ITERS + 1, NC, 8, 128), F32),
            pltpu.VMEM((GROUP, TILES, 128), F32),
            pltpu.VMEM((ITERS - 1, GROUP, TILES, 128), BF16),
            pltpu.VMEM((NY, 8, 128), F32),
            pltpu.VMEM((NC, TILES, 128), F32),
            pltpu.VMEM((2, 8, 128), F32),
            pltpu.VMEM((2, 2, 4 * SHARE, WIDTH), BF16),
            pltpu.VMEM((2, NZ, SHARE, WIDTH), BF16),
            dma((3,)),
            dma((1,)), dma((1,)),
            dma((1,)), dma((1,)), dma((NX,)), dma((NY,)),
            dma((1,)), dma((1,)), dma((NY,)), dma((NY,)),
            dma((1,)), dma((NZ,)),
            dma((1,)), dma((NZ,)),
            dma((ITERS + 1,)), dma((ITERS + 1,)),
            dma((ITERS + 1,)), dma((ITERS + 1,)),
            dma((ITERS,)), dma((ITERS,)),
            dma((1,)), dma((1,)),
            dma((1,)), dma((1,)),
            dma((2,)), dma((2,)),
            dma((1,)), dma((1,)),
        ],
        compiler_params=pltpu.CompilerParams(
            collective_id=0, has_side_effects=True, vmem_limit_bytes=55172 * 1024),
        name="sinkhorn",
    )(noise_latents, teacher_latent_rows.T)
    row_pot, col_pot, targets = pl.pallas_call(
        give,
        out_shape=shapes,
        in_specs=[vmem, vmem, vmem],
        out_specs=(hbm, hbm, hbm),
        scratch_shapes=[dma((3,))],
        compiler_params=pltpu.CompilerParams(vmem_limit_bytes=2**20),
        name="give",
    )(*results)
    return row_pot.reshape(2048), col_pot.reshape(1024), targets


def solution(mesh):
    return jax.shard_map(
        shards,
        mesh=mesh,
        in_specs=(P(("noise", "sample"), None), P("sample", "noise")),
        out_specs=(P("noise"), P("sample"), P(("noise", "sample"), None)),
        check_vma=False,
    )
```
